32 devices in a mesh: head: 8 (over z, core), mlp: 4 (over y, x).
Axes of the slice: x: 2, y: 2, z: 4, core: 2. Of those that a mesh axis runs over, the one named last changes fastest.
Arguments:
- tokens: bfloat16 [4, 1024, 2048], P('mlp', 'head'), may hold values from -6 to 6
- out_grad: bfloat16 [4, 1024, 2048], P('mlp', 'head'), may hold values from -6 to 6
- seq_lengths: int32 [4, 6], P('mlp'), may hold values from 1 to 57, as said below
- norm_gain: bfloat16 [2048], replicated, may hold values from 0.5 to 1.5
- in_weight: bfloat16 [2048, 4, 2048], P(None, None, 'head'), may hold values from -0.125 to 0.125
- rate_weight: bfloat16 [2048, 32], P(None, 'head'), may hold values from -0.125 to 0.125
- init_state: bfloat16 [32, 64, 64], P('head'), may hold values from -0.75 to 0.75
- mix_gain: bfloat16 [2048], P('head'), may hold values from 0.5 to 1.5
- mix_bias: bfloat16 [2048], P('head'), may hold values from -1.5 to 1.5
- out_weight: bfloat16 [2048, 2048], P('head'), may hold values from -0.125 to 0.125
- mlp_gain: bfloat16 [2048], replicated, may hold values from 0.5 to 1.5
- gate_up: bfloat16 [2048, 2, 5504], P(None, None, 'mlp'), may hold values from -0.125 to 0.125
- down_weight: bfloat16 [5504, 2048], P('mlp'), may hold values from -0.078125 to 0.078125
Outputs:
- result: bfloat16 [4, 1024, 2048], P('mlp', 'head')
- grad_tokens: float32 [4, 1024, 2048], P('mlp', 'head')
- grad_norm_gain: float32 [2048], replicated
- grad_in_weight: float32 [2048, 4, 2048], P(None, None, 'head')
- grad_rate_weight: float32 [2048, 32], P(None, 'head')
- grad_init_state: float32 [32, 64, 64], P('head')
- grad_mix_gain: float32 [2048], P('head')
- grad_mix_bias: float32 [2048], P('head')
- grad_out_weight: float32 [2048, 2048], P('head')
- grad_mlp_gain: float32 [2048], replicated
- grad_gate_up: float32 [2048, 2, 5504], P(None, None, 'mlp')
- grad_down: float32 [5504, 2048], P('mlp')
The draws below stay inside these ranges and needn't reach their ends.
Inputs may be any that keep to these rules, and one draw needn't show every extreme that they name: `seq_lengths`: each row holds the lengths of 6 sequences in steps of 16 tokens, packed in order; a row sums to 64; in every row one sequence has the largest length.
All inputs are finite; a program needn't handle non-finite values.
Results may differ from the reference program's by a relative error of at most 0.025.
Values may be sent and summed in bfloat16 or wider, within the bound.
A program may use at most 256 MiB of HBM per device.

```python
from functools import partial
import jax
import jax.numpy as jnp
from jax import lax

D = 2048
H = 32
HEAD_DIM = 64
FF = 5504
MINIBATCH = 16
SEQS = 6
TOK_DEV = 128
GROUP_TOK = 1024
GROUPS = 4


def draw_seq_lengths(key, part):
    key = jax.random.fold_in(key, 7)
    key_weight = jax.random.fold_in(key, 1)
    key_place = jax.random.fold_in(key, 2)
    per_device = TOK_DEV // MINIBATCH
    per_group = GROUP_TOK // MINIBATCH
    remainder = jnp.full((GROUPS,), per_device - 1, jnp.int32)
    weights = jax.random.randint(key_weight, (GROUPS, SEQS - 1), 1, 9)
    weights = weights * weights * weights
    surplus = remainder - (SEQS - 1)
    shares = 1 + surplus[:, None] * weights // jnp.sum(weights, axis=1, keepdims=True)
    shares = shares.at[:, 0].add(remainder - jnp.sum(shares, axis=1))
    longest = per_group - remainder
    placement = jax.random.randint(key_place, (GROUPS, 1), 0, SEQS)
    positions = jnp.arange(SEQS, dtype=jnp.int32)[None, :]
    shorter_at = jnp.clip(positions - (positions > placement).astype(jnp.int32), 0, SEQS - 2)
    gathered = jnp.take_along_axis(shares, shorter_at, axis=1)
    return jnp.where(positions == placement, longest[:, None], gathered).astype(jnp.int32)


def block_levels(stream_key, shape, cuts, least, top_value):
    def one(axis_at, shards_of):
        heights = jax.random.uniform(jax.random.fold_in(jax.random.fold_in(stream_key, 6), axis_at), (shards_of,), jnp.float32, least / len(cuts), top_value / len(cuts))
        return jnp.repeat(jnp.exp(heights), shape[axis_at] // shards_of).reshape((-1,) + (1,) * (len(shape) - axis_at - 1))

    loudness = one(*cuts[0])
    for cut in cuts[1:]:
        loudness = loudness * one(*cut)
    return loudness


def scatter_about(key, extent, width, most, pieces=(), kind=jnp.bfloat16):
    array = width * jax.random.normal(key, extent, jnp.float32)
    if pieces:
        array = array * block_levels(key, extent, pieces, -0.22, 0.18)
    return jnp.clip(array, -most, most).astype(kind)


def setup_inputs(seed: int = 0) -> dict:
    key_of = jax.random.split(jax.random.key(seed), 14)
    return {
        "tokens": scatter_about(key_of[0], (GROUPS, GROUP_TOK, D), 1.0, 6.0, ((0, 4), (1, 8))),
        "out_grad": scatter_about(key_of[1], (GROUPS, GROUP_TOK, D), 1.0, 6.0, ((0, 4), (1, 8))),
        "seq_lengths": draw_seq_lengths(jax.random.fold_in(key_of[13], 71), 0),
        "norm_gain": jnp.clip(1.0 + 0.1 * jax.random.normal(key_of[3], (D,), jnp.float32), 0.5, 1.5).astype(jnp.bfloat16),
        "in_weight": scatter_about(key_of[4], (D, 4, D), D ** -0.5, 0.125, ((2, 8),)),
        "rate_weight": scatter_about(key_of[5], (D, H), D ** -0.5, 0.125, ((1, 8),)),
        "init_state": scatter_about(key_of[6], (H, HEAD_DIM, HEAD_DIM), HEAD_DIM ** -0.5, 0.75, ((0, 8),)),
        "mix_gain": jnp.clip(1.0 + 0.1 * jax.random.normal(key_of[7], (D,), jnp.float32), 0.5, 1.5).astype(jnp.bfloat16),
        "mix_bias": scatter_about(key_of[8], (D,), 0.3, 1.5, ((0, 8),)),
        "out_weight": scatter_about(key_of[9], (D, D), D ** -0.5, 0.125, ((0, 8),)),
        "mlp_gain": jnp.clip(1.0 + 0.1 * jax.random.normal(key_of[10], (D,), jnp.float32), 0.5, 1.5).astype(jnp.bfloat16),
        "gate_up": scatter_about(key_of[11], (D, 2, FF), D ** -0.5, 0.125, ((2, 4),)),
        "down_weight": scatter_about(key_of[12], (FF, D), FF ** -0.5, 0.078125, ((0, 4),)),
    }


PRECISE = lax.Precision.HIGHEST

@jax.custom_vjp
def low(v):
    return lax.optimization_barrier(v.astype(jnp.bfloat16)).astype(jnp.float32)

@jax.custom_vjp
def low_back(v):
    return v

def low_keep(v):
    return (low(v), None)

def low_pass(kept, grad):
    return (grad,)

def back_keep(v):
    return (v, None)

def back_low(kept, grad):
    return (low(grad),)
low.defvjp(low_keep, low_pass)
low_back.defvjp(back_keep, back_low)

def matmul_high(left, right):
    return jnp.dot(left, right, precision=PRECISE)

def rms_scale(values):
    return lax.rsqrt(lax.optimization_barrier(jnp.mean(values * values, axis=-1, keepdims=True)) + 1e-06)

def resets_of(lengths_row, block_count):
    end_marks = jnp.cumsum(lengths_row)
    starts = end_marks - lengths_row
    positions = jnp.arange(block_count, dtype=jnp.int32)
    return jnp.any(positions[:, None] == starts[None, :].astype(jnp.int32), axis=1).astype(jnp.float32)

def mixer(triple, gate_pre, rate_logit, initial, gains, biases, reset_flags):
    row_count = triple.shape[0]
    feature_width = triple.shape[2]
    head_count = feature_width // HEAD_DIM
    blocks = row_count // MINIBATCH
    split_rows = triple.reshape(blocks, MINIBATCH, 3, head_count, HEAD_DIM)
    step_rates = (jax.nn.sigmoid(rate_logit) / (MINIBATCH * HEAD_DIM)).reshape(blocks, MINIBATCH, head_count)
    positions = jnp.arange(MINIBATCH)
    causal = (positions[:, None] >= positions[None, :]).astype(jnp.float32)

    def advance(inner_state, scan_item):
        block_item, step_rate, reset_flag = scan_item
        inner_state = reset_flag * initial + (1.0 - reset_flag) * inner_state
        queries = block_item[:, 0]
        key_rows = block_item[:, 1]
        values = block_item[:, 2]
        residue = jnp.einsum('thi,hij->thj', key_rows, inner_state, precision=PRECISE) - values
        scores = jnp.einsum('thi,shi->hts', queries, key_rows, precision=PRECISE)
        scores = scores * causal[None] * step_rate.T[:, None, :]
        inner_out = jnp.einsum('thi,hij->thj', queries, inner_state, precision=PRECISE)
        inner_out = inner_out - jnp.einsum('hts,shj->thj', scores, residue, precision=PRECISE)
        inner_state = inner_state - jnp.einsum('shi,sh,shj->hij', key_rows, step_rate, residue, precision=PRECISE)
        return (inner_state, inner_out)
    zero_state = jnp.zeros((head_count, HEAD_DIM, HEAD_DIM), jnp.float32)
    _, block_outs = lax.scan(jax.checkpoint(advance), zero_state, (split_rows, step_rates, reset_flags))
    inner_out = block_outs.reshape(row_count, head_count, HEAD_DIM)
    centered = inner_out - lax.optimization_barrier(jnp.mean(inner_out, axis=2, keepdims=True))
    normed = centered * lax.rsqrt(lax.optimization_barrier(jnp.mean(centered * centered, axis=2, keepdims=True)) + 1e-06)
    normed = normed.reshape(row_count, feature_width) * gains + biases
    return normed * jax.nn.gelu(gate_pre)

def group_forward(weight_set, scan_item):
    norm_gain, in_weight, rate_weight, init_state, mix_gain, mix_bias, out_weight, mlp_gain, gate_up, down_weight = weight_set
    rows_in, reset = scan_item
    normed = low(rows_in * rms_scale(rows_in) * norm_gain)
    projected = matmul_high(normed, in_weight.reshape(D, 4 * D)).reshape(-1, 4, D)
    triple = low(low_back(projected[:, :3]))
    gate_pre = low_back(projected[:, 3])
    rate_logit = low_back(matmul_high(normed, rate_weight))
    mixed = low(low_back(mixer(triple, gate_pre, rate_logit, init_state, mix_gain, mix_bias, reset)))
    branch = low_back(matmul_high(mixed, out_weight))
    hidden = rows_in + branch
    normed2 = low(hidden * rms_scale(hidden) * mlp_gain)
    gate_up_pre = low_back(matmul_high(normed2, gate_up.reshape(D, 2 * FF)).reshape(-1, 2, FF))
    activation = low(jax.nn.silu(gate_up_pre[:, 0]) * gate_up_pre[:, 1])
    return hidden + matmul_high(activation, down_weight)

def reference(tokens, out_grad, seq_lengths, norm_gain, in_weight, rate_weight, init_state, mix_gain, mix_bias, out_weight, mlp_gain, gate_up, down_weight):
    block_count = GROUP_TOK // MINIBATCH
    resets = jax.vmap(partial(resets_of, block_count=block_count))(seq_lengths)
    params = tuple((parameter.astype(jnp.float32) for parameter in (norm_gain, in_weight, rate_weight, init_state, mix_gain, mix_bias, out_weight, mlp_gain, gate_up, down_weight)))

    def forward(rows_all, weight_set):
        return lax.map(jax.checkpoint(partial(group_forward, weight_set)), (rows_all, resets))
    result, pullback = jax.vjp(forward, tokens.astype(jnp.float32), params)
    grad_tokens, grads = pullback(out_grad.astype(jnp.float32))
    return (result.astype(jnp.bfloat16), grad_tokens, grads[0], grads[1], grads[2], grads[3], grads[4], grads[5], grads[6], grads[7], grads[8], grads[9])
```

```python
import jax
import jax.numpy as jnp
from jax import lax
from jax.experimental import pallas as pl
from jax.experimental.pallas import tpu as pltpu
from jax.sharding import PartitionSpec as P

HEAD_DIM = 64
MINIBATCH = 16
CHUNK = 128
LANES = 128
VMEM_MOST = 62 * 1024 * 1024
PAIR = LANES // HEAD_DIM
F32 = jnp.float32
BF16 = jnp.bfloat16


def mm(left, right):
    return jnp.dot(left.astype(BF16), right.astype(BF16), preferred_element_type=F32)


def mm_nt(left, right):
    return lax.dot_general(
        left.astype(BF16), right.astype(BF16), (((1,), (1,)), ((), ())), preferred_element_type=F32
    )


def mm_tn(left, right):
    return lax.dot_general(
        left.astype(BF16), right.astype(BF16), (((0,), (0,)), ((), ())), preferred_element_type=F32
    )


def mm_split(left, right):
    high = left.astype(BF16)
    rest = (left - high.astype(F32)).astype(BF16)
    return mm(high, right) + mm(rest, right)


def chunk_masks(len_ref, chunk):
    steps = CHUNK // MINIBATCH
    base = chunk * steps
    row = lax.broadcasted_iota(jnp.int32, (CHUNK, CHUNK), 0)
    col = lax.broadcasted_iota(jnp.int32, (CHUNK, CHUNK), 1)
    row_step = row // MINIBATCH
    col_step = col // MINIBATCH
    row_seq = jnp.zeros((CHUNK, CHUNK), jnp.int32)
    col_seq = jnp.zeros((CHUNK, CHUNK), jnp.int32)
    before = jnp.int32(0)
    last = jnp.int32(0)
    start = jnp.int32(0)
    for at in range(len_ref.shape[1]):
        edge = start - base
        row_seq += (row_step >= edge).astype(jnp.int32)
        col_seq += (col_step >= edge).astype(jnp.int32)
        before += (edge <= -1).astype(jnp.int32)
        last += (edge <= steps - 1).astype(jnp.int32)
        start = start + len_ref[0, at]
    same = row_seq == col_seq
    earlier = jnp.where(same & (col_step < row_step), 1.0, 0.0).astype(F32)
    causal = jnp.where(same & (col <= row), 1.0, 0.0).astype(F32)
    carried = jnp.where(row_seq == before, 1.0, 0.0).astype(F32)
    final = jnp.where(row_seq == last, 1.0, 0.0).astype(F32)
    keep = jnp.where(before == last, 1.0, 0.0).astype(F32)
    return earlier, causal, carried, final, keep


def half_masks():
    lane = lax.broadcasted_iota(jnp.int32, (CHUNK, LANES), 1)
    return [jnp.where(lane // HEAD_DIM == at, 1.0, 0.0).astype(BF16) for at in range(PAIR)]


def same_head(dtype):
    row = lax.broadcasted_iota(jnp.int32, (LANES, LANES), 0) // HEAD_DIM
    col = lax.broadcasted_iota(jnp.int32, (LANES, LANES), 1) // HEAD_DIM
    return jnp.where(row == col, 1.0, 0.0).astype(dtype)


def spread_pair(first, second):
    zero = jnp.zeros((HEAD_DIM, HEAD_DIM), F32)
    return jnp.concatenate(
        [
            jnp.concatenate([first, zero], axis=1),
            jnp.concatenate([zero, second], axis=1),
        ],
        axis=0,
    )


def rates_of(proj_ref, width):
    return jax.nn.sigmoid(proj_ref[:, 4 * width : 4 * width + LANES])


def spread_rate(rates, pair):
    lane = lax.broadcasted_iota(jnp.int32, (CHUNK, LANES), 1)
    first = rates[:, PAIR * pair : PAIR * pair + 1]
    second = rates[:, PAIR * pair + 1 : PAIR * pair + 2]
    return jnp.where(lane < HEAD_DIM, first, second) * (1.0 / (MINIBATCH * HEAD_DIM))


GELU_A = 0.7978845608028654
GELU_B = 0.044715


def gelu_parts(x):
    square = x * x
    bend = jnp.tanh(GELU_A * x * (1.0 + GELU_B * square))
    half = 0.5 * (1.0 + bend)
    slope = half + 0.5 * x * (1.0 - bend * bend) * GELU_A * (1.0 + 3.0 * GELU_B * square)
    return x * half, slope


def scaled_parts(proj_ref, pair, width, rates):
    def part(at):
        return proj_ref[:, at * width + pair * LANES : at * width + (pair + 1) * LANES]

    query = part(0).astype(BF16)
    key = part(1).astype(BF16)
    scaled_key = (key.astype(F32) * spread_rate(rates, pair)).astype(BF16)
    return query, key, scaled_key, part


def forward_local(len_ref, proj_ref, t_ref, a_ref, chunk):
    heads = t_ref.shape[1]
    width = heads * HEAD_DIM
    earlier, causal, _, _, _ = chunk_masks(len_ref, chunk)
    halves = half_masks()
    rates = rates_of(proj_ref, width)
    for pair in range(heads // PAIR):
        query, key, scaled_key, _ = scaled_parts(proj_ref, pair, width, rates)
        for at in range(PAIR):
            head = PAIR * pair + at
            one = -earlier * mm_nt(key * halves[at], scaled_key)
            a_ref[0, head] = (causal * mm_nt(query * halves[at], scaled_key)).astype(BF16)
            one_low = one.astype(BF16)
            two = mm(one_low, one_low)
            two_low = two.astype(BF16)
            total = one + two + mm(two_low, one_low)
            four = mm(two_low, two_low)
            t_ref[0, head] = (total + four + mm(four, total)).astype(BF16)


def forward_state(len_ref, proj_ref, init_ref, e_ref, z_ref, s_ref, t_ref, a_ref, state, first, chunk):
    pairs = state.shape[0]
    width = pairs * LANES

    @pl.when(chunk == 0)
    def _():
        for pair in range(pairs):
            spread = spread_pair(
                init_ref[PAIR * pair].astype(F32), init_ref[PAIR * pair + 1].astype(F32)
            )
            first[pair] = spread
            state[pair] = spread

    _, _, carried, final, keep = chunk_masks(len_ref, chunk)
    halves = half_masks()
    block = same_head(F32)
    rates = rates_of(proj_ref, width)
    outs = []
    for pair in range(pairs):
        lanes = slice(pair * LANES, (pair + 1) * LANES)
        query, key, scaled_key, part = scaled_parts(proj_ref, pair, width, rates)
        value = part(2).astype(BF16).astype(F32)
        now = state[pair]
        start = first[pair]
        both = jnp.concatenate([now, start], axis=1).astype(BF16)
        s_ref[0, pair] = now.astype(BF16)
        key_state = mm(key, both)
        query_state = mm(query, both)
        target = jnp.where(carried > 0.5, key_state[:, :LANES], key_state[:, LANES:]) - value
        target_low = target.astype(BF16)
        error = target
        for at in range(PAIR):
            error = error + mm(t_ref[0, PAIR * pair + at], target_low * halves[at])
        error_low = error.astype(BF16)
        e_ref[:, lanes] = error_low
        state[pair] = (
            keep * now + (1.0 - keep) * start - block * mm_tn(scaled_key * final.astype(BF16), error_low)
        )
        out = jnp.where(carried > 0.5, query_state[:, :LANES], query_state[:, LANES:])
        for at in range(PAIR):
            out = out - mm(a_ref[0, PAIR * pair + at], error_low * halves[at])
        z_ref[:, lanes] = out
        outs.append(out)
    return outs


def forward_tail(outs, gates, gain_ref, bias_ref, mixed_ref):
    mean = same_head(BF16) * (1.0 / HEAD_DIM)
    for pair, out in enumerate(outs):
        lanes = slice(pair * LANES, (pair + 1) * LANES)
        centered = out - mm_split(out, mean)
        normed = centered * lax.rsqrt(mm_split(centered * centered, mean) + 1e-06)
        gelu, _ = gelu_parts(gates[:, lanes])
        mixed_ref[:, lanes] = ((normed * gain_ref[:, lanes] + bias_ref[:, lanes]) * gelu).astype(BF16)


def forward_kernel(len_ref, proj_ref, init_ref, gain_ref, bias_ref, mixed_ref, e_ref, z_ref, s_ref, t_ref, a_ref, state, first):
    chunk = pl.program_id(0)
    width = mixed_ref.shape[1]
    forward_local(len_ref, proj_ref, t_ref, a_ref, chunk)
    outs = forward_state(
        len_ref, proj_ref, init_ref, e_ref, z_ref, s_ref, t_ref, a_ref, state, first, chunk
    )
    forward_tail(outs, proj_ref[:, 3 * width : 4 * width], gain_ref, bias_ref, mixed_ref)


def backward_kernel(
    len_ref, dm_ref, proj_ref, init_ref, gain_ref, bias_ref, e_ref, z_ref, s_ref, t_ref, a_ref,
    dproj_ref, dinit_ref, dgain_ref, dbias_ref, grad, first, dfirst,
):
    step = pl.program_id(0)
    chunks = pl.num_programs(0)
    chunk = chunks - 1 - step
    pairs = grad.shape[0]
    width = pairs * LANES

    @pl.when(step == 0)
    def _():
        for pair in range(pairs):
            first[pair] = spread_pair(
                init_ref[PAIR * pair].astype(F32), init_ref[PAIR * pair + 1].astype(F32)
            ).astype(BF16)
        grad[...] = jnp.zeros_like(grad)
        dfirst[...] = jnp.zeros_like(dfirst)
        dgain_ref[...] = jnp.zeros_like(dgain_ref)
        dbias_ref[...] = jnp.zeros_like(dbias_ref)

    earlier, causal, carried, final, keep = chunk_masks(len_ref, chunk)
    halves = half_masks()
    block = same_head(F32)
    mean = same_head(BF16) * (1.0 / HEAD_DIM)
    rates = rates_of(proj_ref, width)
    drate = jnp.zeros((CHUNK, LANES), F32)
    for pair in range(pairs):
        lanes = slice(pair * LANES, (pair + 1) * LANES)

        def spot(at):
            return slice(at * width + pair * LANES, at * width + (pair + 1) * LANES)

        query = proj_ref[:, spot(0)].astype(BF16)
        key = proj_ref[:, spot(1)].astype(BF16)
        gate = proj_ref[:, spot(3)]
        rate = spread_rate(rates, pair)
        key_wide = key.astype(F32)
        scaled_key = (key_wide * rate).astype(BF16)
        out = z_ref[:, lanes]
        centered = out - mm_split(out, mean)
        scale = lax.rsqrt(mm_split(centered * centered, mean) + 1e-06)
        normed = centered * scale
        gain = gain_ref[:, lanes]
        gelu, slope = gelu_parts(gate)
        dmixed = dm_ref[:, lanes].astype(F32)
        dy = dmixed * gelu
        dproj_ref[:, spot(3)] = (dmixed * (normed * gain + bias_ref[:, lanes]) * slope).astype(BF16)
        dgain_ref[:, lanes] += jnp.sum(dy * normed, axis=0, keepdims=True)
        dbias_ref[:, lanes] += jnp.sum(dy, axis=0, keepdims=True)
        dnormed = dy * gain
        dout = scale * (dnormed - mm_split(dnormed, mean) - normed * mm_split(dnormed * normed, mean))
        dout_low = dout.astype(BF16)
        error = e_ref[:, lanes]
        upper = grad[pair]
        upper_low = upper.astype(BF16)
        derror = -rate * final * mm(key, upper_low)
        for at in range(PAIR):
            derror = derror - mm_tn(a_ref[0, PAIR * pair + at], dout_low * halves[at])
        derror_low = derror.astype(BF16)
        dtarget = derror
        for at in range(PAIR):
            dtarget = dtarget + mm_tn(t_ref[0, PAIR * pair + at], derror_low * halves[at])
        dtarget_low = dtarget.astype(BF16)
        dproj_ref[:, spot(2)] = (-dtarget).astype(BF16)
        both = jnp.concatenate([s_ref[0, pair], first[pair]], axis=0)
        from_out = mm_nt(dout_low, both)
        from_target = mm_nt(dtarget_low, both)
        dquery = jnp.where(carried > 0.5, from_out[:, :LANES], from_out[:, LANES:])
        dkey = jnp.where(carried > 0.5, from_target[:, :LANES], from_target[:, LANES:])
        dscaled = -final * mm_nt(error, upper_low)
        for at in range(PAIR):
            dscore = (-causal * mm_nt(dout_low * halves[at], error)).astype(BF16)
            dlower = (-earlier * mm_nt(dtarget_low * halves[at], error)).astype(BF16)
            part = scaled_key * halves[at]
            dquery = dquery + mm(dscore, part)
            dkey = dkey + mm(dlower, part)
            dscaled = dscaled + mm_tn(dscore, query * halves[at]) + mm_tn(dlower, key * halves[at])
        dkey = dkey + rate * dscaled
        dproj_ref[:, spot(0)] = dquery.astype(BF16)
        dproj_ref[:, spot(1)] = dkey.astype(BF16)
        row_head = lax.broadcasted_iota(jnp.int32, (LANES, LANES), 0) // HEAD_DIM
        col = lax.broadcasted_iota(jnp.int32, (LANES, LANES), 1)
        pick = jnp.where(col == PAIR * pair + row_head, 1.0, 0.0).astype(BF16)
        drate = drate + mm_split(dscaled * key_wide, pick)
        rows = jnp.concatenate([key, query], axis=0)
        carried_low = carried.astype(BF16)
        carried_both = jnp.concatenate([carried_low, carried_low], axis=0)
        kept = rows * carried_both
        sides = jnp.concatenate([kept, rows - kept], axis=1)
        pulled = mm_tn(sides, jnp.concatenate([dtarget_low, dout_low], axis=0))
        grad[pair] = keep * upper + block * pulled[:LANES]
        dfirst[pair] += (1.0 - keep) * upper + block * pulled[LANES:]
    dproj_ref[:, 4 * width :] = (
        drate * rates * (1.0 - rates) * (1.0 / (MINIBATCH * HEAD_DIM))
    ).astype(BF16)

    @pl.when(step == chunks - 1)
    def _():
        for pair in range(pairs):
            dinit_ref[PAIR * pair] = dfirst[pair, :HEAD_DIM, :HEAD_DIM]
            dinit_ref[PAIR * pair + 1] = dfirst[pair, HEAD_DIM:, HEAD_DIM:]


MESH = pl.DeviceIdType.MESH


def chip_peer(hops):
    me = lax.axis_index("head")
    chips = lax.axis_size("head") // 2
    return {"head": lax.rem(me // 2 + hops, chips) * 2 + lax.rem(me, 2)}


def core_peer():
    me = lax.axis_index("head")
    return {"head": me + 1 - 2 * lax.rem(me, 2)}


def head_peer(ahead):
    return {"head": lax.rem(lax.axis_index("head") + ahead, lax.axis_size("head"))}


def mlp_peer(flip):
    me = lax.axis_index("mlp")
    across, along = lax.rem(me, 2), me // 2
    if flip % 2:
        across = 1 - across
    if flip // 2:
        along = 1 - along
    return {"mlp": 2 * along + across}


def greet(peers):
    barrier = pltpu.get_barrier_semaphore()
    for peer in peers:
        pl.semaphore_signal(barrier, inc=1, device_id=peer, device_id_type=MESH)
    pl.semaphore_wait(barrier, len(peers))


def copies_of(moves, send_sems, recv_sems, base=0):
    made = []
    for at, (source, target, peer) in enumerate(moves, base):
        if peer is None:
            made.append(pltpu.make_async_copy(source, target, send_sems.at[at]))
        else:
            made.append(
                pltpu.make_async_remote_copy(
                    src_ref=source,
                    dst_ref=target,
                    send_sem=send_sems.at[at],
                    recv_sem=recv_sems.at[at],
                    device_id=peer,
                    device_id_type=MESH,
                )
            )
    return made


def launch(moves, send_sems, recv_sems, base=0):
    for copy in copies_of(moves, send_sems, recv_sems, base):
        copy.start()


def settle(moves, send_sems, recv_sems, base=0):
    for copy in copies_of(moves, send_sems, recv_sems, base):
        copy.wait()


def anywhere(count):
    return [pl.BlockSpec(memory_space=pl.ANY)] * count


def sem_pair(count):
    return [pltpu.SemaphoreType.DMA((count,)), pltpu.SemaphoreType.DMA((count,))]


def gather_parts(moves, sems):
    copies = [
        pltpu.make_async_copy(source, target, sems.at[at])
        for at, (source, target) in enumerate(moves)
    ]
    for copy in copies:
        copy.start()
    for copy in copies:
        copy.wait()


def near_peers():
    return [mlp_peer(flip) for flip in (1, 2, 3)]


def line_peers():
    return [chip_peer(hops) for hops in (1, 2, 3)]


def line_moves(values, begin, target):
    size = values.shape[0] // 2
    part = values.at[pl.ds(begin * size, size)]
    peers = line_peers()
    return [(part, target.at[pl.ds(at * size, size)], peers[at]) for at in range(3)]


class Carry:
    def __init__(self, arrays=(), out_shape=(), plan=None, count=1, collective_id=None, later=None):
        self.arrays = list(arrays)
        self.out_shape = [jax.ShapeDtypeStruct(shape, BF16) for shape in out_shape]
        self.plan = plan
        self.count = count
        self.collective_id = collective_id
        self.later = later

    def params(self):
        extra = {}
        if self.plan is not None:
            extra = {"collective_id": self.collective_id, "has_side_effects": True}
        return pltpu.CompilerParams(vmem_limit_bytes=VMEM_MOST, **extra)

    def split(self, refs, ins, outs):
        mine, given = len(self.arrays), len(self.out_shape)
        body = refs[:ins] + refs[ins + mine : ins + mine + outs] + refs[ins + mine + outs + given : -2]
        extra_in = refs[ins : ins + mine]
        extra_out = refs[ins + mine + outs : ins + mine + outs + given]
        return body, extra_in, extra_out, refs[-2], refs[-1]

    def wrap(self, body, ins, outs):
        def kernel(*refs):
            own, extra_in, extra_out, send_sems, recv_sems = self.split(refs, ins, outs)
            if self.plan is not None:

                @pl.when(pl.program_id(0) == 0)
                def _():
                    peers, moves = self.plan(extra_in, extra_out)
                    greet(peers)
                    launch(moves, send_sems, recv_sems)

            if self.later is not None:

                @pl.when(pl.program_id(0) == self.later[0])
                def _():
                    moves = self.plan(extra_in, extra_out)[1]
                    settle(moves[: self.later[1]], send_sems, recv_sems)
                    launch(self.later[2](extra_in, extra_out), send_sems, recv_sems, len(moves))

            body(*own)
            if self.plan is not None:

                @pl.when(pl.program_id(0) == pl.num_programs(0) - 1)
                def _():
                    moves = self.plan(extra_in, extra_out)[1]
                    done = 0 if self.later is None else self.later[1]
                    settle(moves[done:], send_sems, recv_sems, done)
                    if self.later is not None:
                        settle(self.later[2](extra_in, extra_out), send_sems, recv_sems, len(moves))

        return kernel


def mixer_forward(lengths, proj, initial, gains, biases, carry):
    rows = proj.shape[0]
    heads = initial.shape[0]
    width = heads * HEAD_DIM
    chunks = rows // CHUNK
    pairs = heads // PAIR
    full = lambda *shape: pl.BlockSpec(shape, lambda c: (0,) * len(shape))
    got = pl.pallas_call(
        carry.wrap(forward_kernel, 5, 6),
        grid=(chunks,),
        in_specs=[
            pl.BlockSpec(memory_space=pltpu.SMEM),
            pl.BlockSpec((CHUNK, proj.shape[1]), lambda c: (c, 0)),
            full(heads, HEAD_DIM, HEAD_DIM),
            full(1, width),
            full(1, width),
            *anywhere(len(carry.arrays)),
        ],
        out_specs=[
            pl.BlockSpec((CHUNK, width), lambda c: (c, 0)),
            pl.BlockSpec((CHUNK, width), lambda c: (c, 0)),
            pl.BlockSpec((CHUNK, width), lambda c: (c, 0)),
            pl.BlockSpec((1, pairs, LANES, LANES), lambda c: (c, 0, 0, 0)),
            pl.BlockSpec((1, heads, CHUNK, CHUNK), lambda c: (c, 0, 0, 0)),
            pl.BlockSpec((1, heads, CHUNK, CHUNK), lambda c: (c, 0, 0, 0)),
            *anywhere(len(carry.out_shape)),
        ],
        out_shape=[
            jax.ShapeDtypeStruct((rows, width), BF16),
            jax.ShapeDtypeStruct((rows, width), BF16),
            jax.ShapeDtypeStruct((rows, width), F32),
            jax.ShapeDtypeStruct((chunks, pairs, LANES, LANES), BF16),
            jax.ShapeDtypeStruct((chunks, heads, CHUNK, CHUNK), BF16),
            jax.ShapeDtypeStruct((chunks, heads, CHUNK, CHUNK), BF16),
            *carry.out_shape,
        ],
        scratch_shapes=[
            pltpu.VMEM((pairs, LANES, LANES), F32),
            pltpu.VMEM((pairs, LANES, LANES), F32),
            *sem_pair(carry.count),
        ],
        compiler_params=carry.params(),
        cost_estimate=pl.CostEstimate(
            flops=rows * width * CHUNK * 40, bytes_accessed=rows * width * 30, transcendentals=rows * width
        ),
        name="mixer_forward",
    )(lengths, proj, initial, gains, biases, *carry.arrays)
    return got[:6], got[6:]


def mixer_backward(lengths, dmixed, proj, initial, gains, biases, kept, carry, places=(0, 0)):
    rows = proj.shape[0]
    heads = initial.shape[0]
    width = heads * HEAD_DIM
    chunks = rows // CHUNK
    pairs = heads // PAIR
    full = lambda *shape: pl.BlockSpec(shape, lambda i: (0,) * len(shape))
    at = lambda *shape: pl.BlockSpec(shape, lambda i: (chunks - 1 - i,) + (0,) * (len(shape) - 1))
    got = pl.pallas_call(
        carry.wrap(backward_kernel, 11, 4),
        grid=(chunks,),
        in_specs=[
            pl.BlockSpec(memory_space=pltpu.SMEM),
            at(CHUNK, width),
            at(CHUNK, proj.shape[1]),
            full(heads, HEAD_DIM, HEAD_DIM),
            pl.BlockSpec((1, width), lambda i: (0, places[0])),
            pl.BlockSpec((1, width), lambda i: (0, places[1])),
            at(CHUNK, width),
            at(CHUNK, width),
            at(1, pairs, LANES, LANES),
            at(1, heads, CHUNK, CHUNK),
            at(1, heads, CHUNK, CHUNK),
            *anywhere(len(carry.arrays)),
        ],
        out_specs=[
            at(CHUNK, proj.shape[1]),
            full(heads, HEAD_DIM, HEAD_DIM),
            full(1, width),
            full(1, width),
            *anywhere(len(carry.out_shape)),
        ],
        out_shape=[
            jax.ShapeDtypeStruct(proj.shape, BF16),
            jax.ShapeDtypeStruct((heads, HEAD_DIM, HEAD_DIM), F32),
            jax.ShapeDtypeStruct((1, width), F32),
            jax.ShapeDtypeStruct((1, width), F32),
            *carry.out_shape,
        ],
        scratch_shapes=[
            pltpu.VMEM((pairs, LANES, LANES), F32),
            pltpu.VMEM((pairs, LANES, LANES), BF16),
            pltpu.VMEM((pairs, LANES, LANES), F32),
            *sem_pair(carry.count),
        ],
        compiler_params=carry.params(),
        cost_estimate=pl.CostEstimate(
            flops=rows * width * CHUNK * 50, bytes_accessed=rows * width * 40, transcendentals=rows * width
        ),
        name="mixer_backward",
    )(lengths, dmixed, proj, initial, gains, biases, *kept, *carry.arrays)
    return got[:4], got[4:]


def head_kernel(*refs):
    len_ref, tokens, rate_rows, init_ref = refs[:4]
    vectors, (weight_raw, cot, out_weight), refs = refs[4:8], refs[8:11], refs[11:]
    proj_ref, rate, mixed_ref, e_ref, z_ref, s_ref, t_ref, a_ref, gain = refs[:9]
    gathered_ref, cot_got, weight_ref, mixed_rows, out_cross, out_other, cot_line, out_line = refs[9:17]
    held, raw, weight, state, first, slots, line_hold, own_hold = refs[17:25]
    line_send, line_recv, core_send, core_recv, near_send, near_recv, out_send, out_recv = refs[25:33]
    keep_sem, weight_sem, row_send, row_recv, cross_send, cross_recv = refs[33:39]
    cot_send, cot_recv, other_send, other_recv, hold_sems = refs[39:]
    me = lax.axis_index("head")
    chip, core = me // 2, lax.rem(me, 2)
    member = lax.axis_index("mlp")
    rows = tokens.shape[0]
    chips = held.shape[0] // (2 * rows)
    sides = [mlp_peer(flip) for flip in (1, 2, 3)]
    others = [chip_peer(hops) for hops in range(1, chips)]
    partner = core_peer()
    load = pltpu.make_async_copy(weight_raw, raw, weight_sem.at[0])
    load.start()
    place_at = 0
    for vector in vectors:
        values = vector[...].astype(F32)
        for at in range(vector.shape[0]):
            gain[:, place_at : place_at + LANES] = values[at : at + 1, :]
            place_at += LANES
    source = tokens[...].astype(F32)
    own_rows = pl.ds(pl.multiple_of(me * rows, rows), rows)
    held[own_rows, :] = (source * rms_scale(source) * gain[:, : source.shape[1]]).astype(BF16)
    rate[...] = jnp.zeros_like(rate)
    rate[: rate_rows.shape[0], :] = rate_rows[...]
    greet([head_peer(ahead) for ahead in range(1, 8)] + sides)

    def place(of_chip, of_core):
        return held.at[pl.ds(pl.multiple_of((of_chip * 2 + of_core) * rows, rows), rows)]

    def hop(of_chip, step):
        side = (step + 1) // 2
        return pltpu.make_async_remote_copy(
            src_ref=place(of_chip, core),
            dst_ref=place(of_chip, core),
            send_sem=line_send.at[side, of_chip],
            recv_sem=line_recv.at[of_chip],
            device_id={"head": me + 2 * step},
            device_id_type=MESH,
        )

    def across(of_chip, of_core):
        return pltpu.make_async_remote_copy(
            src_ref=place(of_chip, of_core),
            dst_ref=place(of_chip, of_core),
            send_sem=core_send.at[of_chip],
            recv_sem=core_recv.at[of_chip],
            device_id=partner,
            device_id_type=MESH,
        )

    quarter = out_weight.shape[0] // 4
    part = out_weight.at[pl.ds(pl.multiple_of(member * quarter, quarter), quarter)]
    near_moves = [(cot, cot_got.at[at], sides[at]) for at in range(3)]
    out_moves = [(part, out_line.at[chip], peer) for peer in others]
    for step in (-1, 1):

        @pl.when(jnp.logical_and(chip + step >= 0, chip + step < chips))
        def _(step=step):
            hop(chip, step).start()

    across(chip, core).start()
    launch(out_moves, out_send, out_recv)
    launch(near_moves, near_send, near_recv)
    def product(of_chip):
        block = pl.ds(pl.multiple_of(of_chip * 2 * rows, 2 * rows), 2 * rows)
        values = held[block, :]
        wide = weight.shape[1]
        proj_ref[block, :wide] = jnp.dot(values, weight[...], preferred_element_type=F32)
        proj_ref[block, wide:] = mm_nt(values, rate[...])
        pltpu.make_async_copy(held.at[block], gathered_ref.at[block], keep_sem.at[of_chip]).start()

    def turn(at):
        if isinstance(at, int) and at == 0:
            return chip
        if isinstance(at, int) and at == 1:
            return chip + 1 - 2 * lax.rem(chip, 2)
        return at - (2 * at - 3) * (chip // 2)

    def arrive(at):
        of_chip = turn(at)
        pltpu.make_async_remote_copy(
            src_ref=place(of_chip, core),
            dst_ref=place(of_chip, core),
            send_sem=line_send.at[0, of_chip],
            recv_sem=line_recv.at[of_chip],
            device_id=partner,
            device_id_type=MESH,
        ).wait_recv()
        for step in (-1, 1):
            wanted = (of_chip > chip) if step < 0 else (of_chip < chip)

            @pl.when(jnp.logical_and(wanted, jnp.logical_and(chip + step >= 0, chip + step < chips)))
            def _(step=step):
                hop(of_chip, step).start()

        across(of_chip, core).start()

    near = sides
    heads = 2 * chips
    ahead = [lax.rem(chip + hops, 4) for hops in (1, 2, 3)]
    local = mixed_ref.shape[1]
    half = quarter // 2
    top, bottom = pl.ds(0, half), pl.ds(half, half)

    def row_copy(sender, target, stays):
        rel = lax.rem(core + target, 2)
        place_at = mixed_rows.at[rel, :, pl.ds(pl.multiple_of(chip * local, local), local)]
        if stays:
            return pltpu.make_async_copy(slots.at[target], place_at, row_send.at[target])
        return pltpu.make_async_remote_copy(
            src_ref=slots.at[target],
            dst_ref=place_at,
            send_sem=row_send.at[target],
            recv_sem=row_recv.at[sender],
            device_id={"head": target},
            device_id_type=MESH,
        )

    def cross_moves(flip):
        if flip < 2:
            return [
                (out_line.at[of_chip], out_cross.at[of_chip, member], near[flip])
                for of_chip in ahead
            ]
        moves = []
        for of_chip in ahead:
            one = out_cross.at[of_chip, near[0]["mlp"], top]
            two = out_cross.at[of_chip, near[1]["mlp"], bottom]
            moves += [(one, one, near[1]), (two, two, near[0])]
        return moves

    def swap_moves(flip):
        of_member = near[flip]["mlp"]
        return [
            (out_cross.at[of_chip, of_member], out_other.at[of_chip, of_member], partner)
            for of_chip in ahead
        ]

    def hold_moves():
        moves = [(line_hold.at[at], out_cross.at[ahead[at], member], None) for at in range(3)]
        moves += [(line_hold.at[at], out_other.at[ahead[at], member], partner) for at in range(3)]
        return moves + [
            (own_hold, out_cross.at[chip], None),
            (own_hold, out_other.at[chip], partner),
        ]

    cot_moves = line_moves(cot, 0, cot_line)
    own_out = [
        pltpu.make_async_copy(
            out_weight.at[pl.ds(at * quarter, quarter)], own_hold.at[at], hold_sems.at[3 + at]
        )
        for at in range(4)
    ]
    for copy in own_out:
        copy.start()

    def local_part(of_chip):
        for of_core in range(2):
            at = of_chip * 2 + of_core
            block = pl.ds(pl.multiple_of(at * CHUNK, CHUNK), CHUNK)
            one = pl.ds(at, 1)
            forward_local(len_ref, proj_ref.at[block], t_ref.at[one], a_ref.at[one], at)

    inner = jnp.logical_and(chip > 0, chip < chips - 1)
    outer = jnp.logical_not(inner)
    arrive(1)
    pl.when(inner)(lambda: arrive(2))
    load.wait()
    wide = raw.shape[2]

    def untie(at, _):
        span = pl.ds(pl.multiple_of(at * 256, 256), 256)
        values = raw[span]
        for part in range(4):
            weight[span, part * wide : (part + 1) * wide] = values[:, part, :]
        return 0

    lax.fori_loop(0, raw.shape[0] // 256, untie, 0)
    store = pltpu.make_async_copy(weight, weight_ref, weight_sem.at[1])
    store.start()

    def gather_step(at, _):
        pl.when(jnp.logical_and(inner, at == 1))(lambda: arrive(3))
        pl.when(jnp.logical_and(outer, at == 2))(lambda: arrive(2))
        pl.when(jnp.logical_and(outer, at == 3))(lambda: arrive(3))

        @pl.when(at == 2)
        def _():
            settle(out_moves, out_send, out_recv)
            for flip in range(2):
                launch(cross_moves(flip), cross_send.at[flip], cross_recv.at[flip])
            gather_parts(
                [(out_line.at[ahead[spot]], line_hold.at[spot]) for spot in range(3)], hold_sems
            )
            for copy in own_out:
                copy.wait()
            launch(hold_moves(), other_send.at[3], other_recv.at[3])

        @pl.when(at == 3)
        def _():
            launch(cot_moves, cot_send, cot_recv)

        of_chip = jnp.where(at == 0, turn(0), jnp.where(at == 1, turn(1), turn(at)))
        across(of_chip, 1 - core).wait_recv()
        product(of_chip)
        local_part(of_chip)
        return 0

    lax.fori_loop(0, chips, gather_step, 0)

    def rows_of(at):
        return pl.ds(pl.multiple_of(at * CHUNK, CHUNK), CHUNK)

    def advance(at):
        block, one = rows_of(at), pl.ds(at, 1)
        return forward_state(
            len_ref,
            proj_ref.at[block],
            init_ref,
            e_ref.at[block],
            z_ref.at[block],
            s_ref.at[one],
            t_ref.at[one],
            a_ref.at[one],
            state,
            first,
            at,
        )

    spot = 2 * tokens.shape[1]
    mix_gain = gain.at[:, pl.ds(spot, local)]
    mix_bias = gain.at[:, pl.ds(spot + local, local)]

    def ship(at):
        mixed_ref[rows_of(at), :] = slots[at]

        @pl.when(at != me)
        def _():
            row_copy(me, at, False).start()

        @pl.when(at == me)
        def _():
            row_copy(me, at, True).start()

    def step(at, outs):
        @pl.when(at == 1)
        def _():
            for flip in range(2):
                settle(cross_moves(flip), cross_send.at[flip], cross_recv.at[flip])
            launch(cross_moves(2), cross_send.at[2], cross_recv.at[2])
            for flip in range(2):
                launch(swap_moves(flip), other_send.at[flip], other_recv.at[flip])

        gates = proj_ref[rows_of(at - 1), 3 * local : 4 * local]
        later = advance(at)
        forward_tail(outs, gates, mix_gain, mix_bias, slots.at[at - 1])
        ship(at - 1)
        return tuple(later)

    outs = lax.fori_loop(1, heads, step, tuple(advance(0)))
    gates = proj_ref[rows_of(heads - 1), 3 * local : 4 * local]
    forward_tail(outs, gates, mix_gain, mix_bias, slots.at[heads - 1])
    ship(heads - 1)
    settle(cross_moves(2), cross_send.at[2], cross_recv.at[2])
    launch(swap_moves(2), other_send.at[2], other_recv.at[2])
    settle(cot_moves, cot_send, cot_recv)
    settle(hold_moves(), other_send.at[3], other_recv.at[3])
    for at in range(8):

        @pl.when(me != at)
        def _(at=at):
            row_copy(me, at, False).wait_send()
            row_copy(at, at, False).wait_recv()

        @pl.when(me == at)
        def _(at=at):
            row_copy(me, at, True).wait()

    for at in range(chips):
        of_chip = turn(at)
        across(of_chip, core).wait_send()
        block = pl.ds(pl.multiple_of(of_chip * 2 * rows, 2 * rows), 2 * rows)
        pltpu.make_async_copy(held.at[block], gathered_ref.at[block], keep_sem.at[of_chip]).wait()
        for step in (-1, 1):
            wanted = (of_chip >= chip) if step < 0 else (of_chip <= chip)

            @pl.when(jnp.logical_and(wanted, jnp.logical_and(chip + step >= 0, chip + step < chips)))
            def _(step=step):
                hop(of_chip, step).wait_send()

    settle(near_moves, near_send, near_recv)
    store.wait()
    for flip in range(3):
        settle(swap_moves(flip), other_send.at[flip], other_recv.at[flip])


def head(lengths, tokens, rate_rows, initial, vectors, in_weight, cot, out_weight, collective_id):
    devices = lax.axis_size("head")
    rows, width = tokens.shape
    heads = initial.shape[0]
    local = heads * HEAD_DIM
    pairs = heads // PAIR
    wide = 4 * in_weight.shape[2]
    chips = devices // 2
    quarters = (4, out_weight.shape[0] // 4, width)
    vmem = pl.BlockSpec(memory_space=pltpu.VMEM)
    got = pl.pallas_call(
        head_kernel,
        in_specs=[pl.BlockSpec(memory_space=pltpu.SMEM)] + [vmem] * 7 + anywhere(3),
        out_specs=[vmem] * 9 + anywhere(8),
        out_shape=[
            jax.ShapeDtypeStruct((devices * rows, wide + LANES), F32),
            jax.ShapeDtypeStruct((LANES, width), BF16),
            jax.ShapeDtypeStruct((devices * rows, local), BF16),
            jax.ShapeDtypeStruct((devices * rows, local), BF16),
            jax.ShapeDtypeStruct((devices * rows, local), F32),
            jax.ShapeDtypeStruct((devices, pairs, LANES, LANES), BF16),
            jax.ShapeDtypeStruct((devices, heads, CHUNK, CHUNK), BF16),
            jax.ShapeDtypeStruct((devices, heads, CHUNK, CHUNK), BF16),
            jax.ShapeDtypeStruct((1, sum(vector.size for vector in vectors)), F32),
            jax.ShapeDtypeStruct((devices * rows, width), BF16),
            jax.ShapeDtypeStruct((3, rows, width), BF16),
            jax.ShapeDtypeStruct((width, wide), BF16),
            jax.ShapeDtypeStruct((2, rows, width // 2), BF16),
            jax.ShapeDtypeStruct((4, *quarters), BF16),
            jax.ShapeDtypeStruct((4, *quarters), BF16),
            jax.ShapeDtypeStruct((3 * rows // 2, width), BF16),
            jax.ShapeDtypeStruct((chips, *quarters[1:]), BF16),
        ],
        scratch_shapes=[
            pltpu.VMEM((devices * rows, width), BF16),
            pltpu.VMEM(in_weight.shape, BF16),
            pltpu.VMEM((width, wide), BF16),
            pltpu.VMEM((pairs, LANES, LANES), F32),
            pltpu.VMEM((pairs, LANES, LANES), F32),
            pltpu.VMEM((devices, CHUNK, local), BF16),
            pltpu.VMEM((3, *quarters[1:]), BF16),
            pltpu.VMEM(quarters, BF16),
            pltpu.SemaphoreType.DMA((2, chips)),
            pltpu.SemaphoreType.DMA((chips,)),
            pltpu.SemaphoreType.DMA((chips,)),
            pltpu.SemaphoreType.DMA((chips,)),
            *sem_pair(3),
            *sem_pair(3),
            pltpu.SemaphoreType.DMA((chips,)),
            pltpu.SemaphoreType.DMA((2,)),
            *sem_pair(8),
            pltpu.SemaphoreType.DMA((3, 6)),
            pltpu.SemaphoreType.DMA((3, 6)),
            *sem_pair(3),
            pltpu.SemaphoreType.DMA((4, 8)),
            pltpu.SemaphoreType.DMA((4, 8)),
            pltpu.SemaphoreType.DMA((7,)),
        ],
        compiler_params=pltpu.CompilerParams(
            vmem_limit_bytes=VMEM_MOST, collective_id=collective_id, has_side_effects=True
        ),
        cost_estimate=pl.CostEstimate(
            flops=2 * devices * rows * width * wide, bytes_accessed=4 * devices * rows * width, transcendentals=0
        ),
        name="head",
    )(lengths, tokens, rate_rows, initial, *vectors, in_weight, cot, out_weight)
    return got[:2], got[2:8], got[8], got[9:16]


UNITS = 704
PLANE_UNITS = 688
SPAN = 512
FINISH = 176


def gated(gate, up):
    sigmoid = jax.nn.sigmoid(gate)
    silu = gate * sigmoid
    return silu, sigmoid + silu * (1.0 - sigmoid)


def tile(*shape):
    return pl.BlockSpec(shape, (lambda i: (0, i, 0)) if len(shape) == 3 else (lambda i: (i, 0)))


def plane_kernel(*refs):
    x_own, x_got, o_own, o_got, gu_ref, down_ref, dx_ref, out_ref = refs[:8]
    act_ref, d_gate_ref, d_up_ref, x_all, o_all, dx_sum, out_sum, turned, sems = refs[8:]
    rows = x_own.shape[0]
    step = pl.program_id(0)
    last = pl.num_programs(0) - 1

    @pl.when(step == 0)
    def _():
        moves = [(x_own, x_all.at[pl.ds(0, rows)]), (o_own, o_all.at[pl.ds(0, rows)])]
        for at in range(3):
            place = pl.ds((at + 1) * rows, rows)
            moves += [(x_got.at[at], x_all.at[place]), (o_got.at[at], o_all.at[place])]
        gather_parts(moves, sems)

    gate = mm_nt(gu_ref[0], x_all[...])
    up = mm_nt(gu_ref[1], x_all[...])
    d_act = mm_nt(down_ref[...], o_all[...])
    silu, slope = gated(gate, up)
    act = (silu * up).astype(BF16)
    d_gate = (d_act * up * slope).astype(BF16)
    d_up = (d_act * silu).astype(BF16)
    act_ref[...] = act
    d_gate_ref[...] = d_gate
    d_up_ref[...] = d_up
    for at, part in enumerate((d_gate, d_up, act)):
        turned[at] = part.T

    def back(at, _):
        span = pl.ds(pl.multiple_of(at * SPAN, SPAN), SPAN)
        dx = mm(turned[0], gu_ref[0, :, span]) + mm(turned[1], gu_ref[1, :, span])
        out = mm(turned[2], down_ref[:, span])

        @pl.when(step == 0)
        def _():
            dx_sum[:, span] = dx
            out_sum[:, span] = out

        @pl.when(step > 0)
        def _():
            dx_sum[:, span] += dx
            out_sum[:, span] += out

        @pl.when(step == last)
        def _():
            for at in range(4):
                place = pl.ds(at * rows, rows)
                dx_ref[at, :, span] = dx_sum[place, span].astype(BF16)
                out_ref[at, :, span] = out_sum[place, span].astype(BF16)

        return 0

    lax.fori_loop(0, x_all.shape[1] // SPAN, back, 0)


def mlp_plane(x_own, x_got, o_own, o_got, gate_up_rows, down_weight, carry):
    rows, width = x_own.shape
    hidden = down_weight.shape[0]
    whole = pl.BlockSpec((4, rows, width), lambda i: (0, 0, 0))
    got = pl.pallas_call(
        carry.wrap(plane_kernel, 6, 5),
        grid=(hidden // PLANE_UNITS,),
        in_specs=anywhere(4)
        + [tile(2, PLANE_UNITS, width), tile(PLANE_UNITS, width)]
        + anywhere(len(carry.arrays)),
        out_specs=[whole, whole]
        + [tile(PLANE_UNITS, 4 * rows)] * 3
        + anywhere(len(carry.out_shape)),
        out_shape=[jax.ShapeDtypeStruct((4, rows, width), BF16)] * 2
        + [jax.ShapeDtypeStruct((hidden, 4 * rows), BF16)] * 3
        + carry.out_shape,
        scratch_shapes=[
            pltpu.VMEM((4 * rows, width), BF16),
            pltpu.VMEM((4 * rows, width), BF16),
            pltpu.VMEM((4 * rows, width), F32),
            pltpu.VMEM((4 * rows, width), F32),
            pltpu.VMEM((3, 4 * rows, PLANE_UNITS), BF16),
            pltpu.SemaphoreType.DMA((8,)),
            *sem_pair(carry.count),
        ],
        compiler_params=carry.params(),
        cost_estimate=pl.CostEstimate(
            flops=48 * rows * hidden * width, bytes_accessed=6 * hidden * width, transcendentals=4 * rows * hidden
        ),
        name="mlp_plane",
    )(x_own, x_got, o_own, o_got, gate_up_rows, down_weight, *carry.arrays)
    return got[:2], got[2:5], got[5:]


def grads_kernel(*refs):
    x_own, x_got, x_far, o_own, o_got, o_far = refs[0], refs[1], refs[2:10], refs[10], refs[11], refs[12:20]
    in_part, out_part, back_part, gu_hbm, down_hbm = refs[20:25]
    plane_acts, small_ref, init_ref = refs[25:28], refs[28], refs[29]
    own_gu, own_down, far_gu, far_down, in_all, out_all = refs[30:36]
    core_got, back_got, back_own, small_out, gains_out, init_out = refs[36:42]
    x_all, o_all, act, d_gate, d_up, gu_ref, down_ref, slots = refs[42:50]
    back_low, back_load, small_got, gains_got, init_got = refs[50:55]
    in_bufs, out_bufs = refs[55:61], refs[61:67]
    load_sems, sum_sems, tile_send, tile_recv, phase_send, phase_recv = refs[67:]
    step = pl.program_id(0)
    rows, width = x_all.shape
    me = lax.axis_index("head")
    chip, core = me // 2, lax.rem(me, 2)
    member = lax.axis_index("mlp")
    partner = core_peer()
    near = near_peers()
    across, along = near[0], near[1]
    others = [head_peer(ahead) for ahead in range(1, 8)]
    hidden = own_gu.shape[1]
    sides = ((in_part, in_all, in_bufs), (out_part, out_all, out_bufs))

    def piece(part, of_member, half):
        size = part.shape[0] // 8
        return part.at[pl.ds(pl.multiple_of(of_member * 2 * size + half * size, size), size)]

    def quick_moves():
        moves = [(back_part.at[:, 1 - core], core_got, partner)]
        for at in range(3):
            moves.append((small_ref, small_got.at[at], near[at]))
            moves.append((init_ref, init_got.at[at], near[at]))
        return moves

    def line_sums():
        moves = [(back_low.at[chip], back_own, None)]
        for hops in range(1, 4):
            moves.append(
                (back_low.at[lax.rem(chip + hops, 4)], back_got.at[hops - 1], chip_peer(hops))
            )
        gains = small_out.at[pl.ds(0, 8)]
        return moves + [(gains, gains_got.at[at], others[at]) for at in range(7)]

    def reduce_one():
        moves = []
        for part, _, (got, _, _, _, _, _) in sides:
            moves.append((piece(part, near[0]["mlp"], 0), got.at[0], across))
            moves.append((piece(part, near[2]["mlp"], 0), got.at[1], across))
            moves.append((piece(part, near[1]["mlp"], 1), got.at[2], along))
            moves.append((piece(part, near[2]["mlp"], 1), got.at[3], along))
        return moves

    def reduce_two():
        moves = []
        for _, _, (_, _, passed, _, got, _) in sides:
            moves += [(passed.at[0], got.at[0], along), (passed.at[1], got.at[1], across)]
        return moves

    def spread_one():
        moves = []
        for _, whole, (_, _, _, _, _, total) in sides:
            moves += [(total, whole.at[member], peer) for peer in (across, along, None)]
        return moves

    def spread_two():
        moves = []
        for _, whole, _ in sides:
            half = whole.shape[1] // 2
            top = whole.at[across["mlp"], pl.ds(0, half)]
            bottom = whole.at[along["mlp"], pl.ds(half, half)]
            moves += [(top, top, along), (bottom, bottom, across)]
        return moves

    phases = [quick_moves, line_sums, reduce_one, reduce_two, spread_one, spread_two]

    def begin(at):
        launch(phases[at](), phase_send.at[at], phase_recv.at[at])

    def end(at):
        settle(phases[at](), phase_send.at[at], phase_recv.at[at])

    near_rows = x_own.shape[0]
    plane_rows = 4 * near_rows
    piece_rows = (rows - plane_rows) // 8
    sizes = (UNITS, hidden - UNITS)

    def weight_moves(at):
        span, size = pl.ds(at * UNITS, sizes[at]), pl.ds(0, sizes[at])
        return [(gu_hbm.at[:, span], gu_ref.at[:, size]), (down_hbm.at[span], down_ref.at[size])]

    def act_moves(at):
        span, size = pl.ds(at * UNITS, sizes[at]), pl.ds(0, sizes[at])
        return [
            (part.at[span], whole.at[size, pl.ds(0, plane_rows)])
            for part, whole in zip(plane_acts, (act, d_gate, d_up))
        ]

    def far_moves(begin, end):
        moves = []
        for at in range(begin, end):
            place = pl.ds(plane_rows + at * piece_rows, piece_rows)
            moves += [(x_far[at], x_all.at[place]), (o_far[at], o_all.at[place])]
        return moves

    def near_moves():
        moves = []
        for own, got, whole in ((x_own, x_got, x_all), (o_own, o_got, o_all)):
            moves.append((own, whole.at[pl.ds(0, near_rows)]))
            for at in range(3):
                moves.append((got.at[at], whole.at[pl.ds((at + 1) * near_rows, near_rows)]))
        return moves

    groups = [far_moves(0, 3), far_moves(3, 6), far_moves(6, 8), near_moves()]
    bases = [5, 11, 17, 21]

    def loads(moves, base):
        return [
            pltpu.make_async_copy(source, target, load_sems.at[base + at])
            for at, (source, target) in enumerate(moves)
        ]

    def fetch(moves, base):
        for copy in loads(moves, base):
            copy.start()

    def fetched(moves, base):
        for copy in loads(moves, base):
            copy.wait()

    def chunk_moves(at, column):
        span, size = pl.ds(at * UNITS, sizes[at]), pl.ds(0, sizes[at])
        columns = pl.ds(pl.multiple_of(column * SPAN, SPAN), SPAN)
        slot = slots.at[lax.rem(column, 2)]
        moves = []
        for gu, down, peer in ((own_gu, own_down, None), (far_gu, far_down, partner)):
            moves += [
                (slot.at[0, size], gu.at[0, span, columns], peer),
                (slot.at[1, size], gu.at[1, span, columns], peer),
                (slot.at[2, size], down.at[span, columns], peer),
            ]
        return moves

    def chunk_sems(at, column):
        place = 4 * at + column
        return tile_send.at[place], tile_recv.at[place]

    @pl.when(step == 0)
    def _():
        fetch(weight_moves(0), 0)
        fetch(groups[0], bases[0])
        greet(near + others)
        begin(0)
        begin(2)
        for at in range(1, 4):
            fetch(groups[at], bases[at])
        fetch(act_moves(0), 2)
        fetched(weight_moves(0), 0)

    @pl.when(step == 1)
    def _():
        fetch(act_moves(1), 2)
        fetched(weight_moves(1), 0)

    def reduce_sums():
        parts = []
        for part, _, (_, own, _, _, _, _) in sides:
            parts.append((piece(part, member, 0), own.at[0]))
            parts.append((piece(part, near[1]["mlp"], 0), own.at[1]))
            parts.append((piece(part, member, 1), own.at[2]))
            parts.append((piece(part, near[0]["mlp"], 1), own.at[3]))
        gather_parts(parts, sum_sems)
        end(2)
        for _, _, (got, own, passed, kept, _, _) in sides:
            for half in range(2):
                kept[half] = own[2 * half].astype(F32) + got[2 * half].astype(F32)
                passed[half] = (
                    own[2 * half + 1].astype(F32) + got[2 * half + 1].astype(F32)
                ).astype(BF16)
        begin(3)

    def reduce_totals():
        end(3)
        for _, _, (_, _, _, kept, got, total) in sides:
            size = total.shape[0] // 2
            for half in range(2):
                total[pl.ds(half * size, size), :] = (kept[half] + got[half].astype(F32)).astype(BF16)
        begin(4)

    def spread_rest():
        end(4)
        begin(5)

    def line_totals():
        end(0)

        def add(at, _):
            gather_parts(
                [(core_got.at[at], back_load.at[0]), (back_part.at[at, core], back_load.at[1])],
                sum_sems,
            )
            back_low[at] = (back_load[0].astype(F32) + back_load[1].astype(F32)).astype(BF16)
            return 0

        lax.fori_loop(0, 4, add, 0)
        total, first = small_ref[...], init_ref[...]
        for at in range(3):
            total = total + small_got[at]
            first = first + init_got[at]
        small_out[...] = total
        init_out[...] = first
        begin(1)

    def ahead(at, _):
        for group in range(3):

            @pl.when(jnp.logical_and(step == 0, at == group))
            def _(group=group):
                fetched(groups[group], bases[group])

        pl.when(jnp.logical_and(step == 0, at == 1))(line_totals)
        pl.when(jnp.logical_and(step == 1, at == 1))(reduce_totals)
        span = pl.ds(pl.multiple_of(plane_rows + at * SPAN, SPAN), SPAN)
        rows_in = x_all[span, :]
        gate = mm_nt(gu_ref[0], rows_in)
        up = mm_nt(gu_ref[1], rows_in)
        d_act = mm_nt(down_ref[...], o_all[span, :])
        silu, slope = gated(gate, up)
        act[:, span] = (silu * up).astype(BF16)
        d_gate[:, span] = (d_act * up * slope).astype(BF16)
        d_up[:, span] = (d_act * silu).astype(BF16)
        return 0

    lax.fori_loop(0, (rows - plane_rows) // SPAN, ahead, 0)

    @pl.when(step == 0)
    def _():
        fetch(weight_moves(1), 0)
        fetched(groups[3], bases[3])
        fetched(act_moves(0), 2)

    @pl.when(step == 1)
    def _():
        fetched(act_moves(1), 2)

    def back(at, _):
        pl.when(jnp.logical_and(step == 0, at == 2))(reduce_sums)
        pl.when(jnp.logical_and(step == 1, at == 3))(spread_rest)

        for of_tile in range(2):

            @pl.when(jnp.logical_and(step == of_tile, at >= 2))
            def _(of_tile=of_tile):
                settle(chunk_moves(of_tile, at - 2), *chunk_sems(of_tile, at - 2))

        @pl.when(jnp.logical_and(step == 1, at < 2))
        def _():
            settle(chunk_moves(0, at + 2), *chunk_sems(0, at + 2))

        span = pl.ds(pl.multiple_of(at * SPAN, SPAN), SPAN)
        columns = x_all[:, span]
        slot = lax.rem(at, 2)
        slots[slot, 0] = mm(d_gate[...], columns).astype(BF16)
        slots[slot, 1] = mm(d_up[...], columns).astype(BF16)
        slots[slot, 2] = mm(act[...], o_all[:, span]).astype(BF16)

        for of_tile in range(2):

            @pl.when(step == of_tile)
            def _(of_tile=of_tile):
                launch(chunk_moves(of_tile, at), *chunk_sems(of_tile, at))

        return 0

    lax.fori_loop(0, width // SPAN, back, 0)

    @pl.when(step == 1)
    def _():
        end(1)
        gains = small_out[0:8, :]
        for at in range(7):
            gains = gains + gains_got[at]
        gains_out[...] = gains
        for at in (2, 3):
            settle(chunk_moves(1, at), *chunk_sems(1, at))
        end(5)


def reduce_buffers(part):
    size, width = part.shape[0] // 8, part.shape[1]
    return [
        pltpu.VMEM((4, size, width), BF16),
        pltpu.VMEM((4, size, width), BF16),
        pltpu.VMEM((2, size, width), BF16),
        pltpu.VMEM((2, size, width), F32),
        pltpu.VMEM((2, size, width), BF16),
        pltpu.VMEM((2 * size, width), BF16),
    ]


def mlp_grads(
    x, o, in_part, out_part, back_part, gate_up_rows, down_weight, plane_acts, small, init, collective_id
):
    arrays = [x[0], x[1], *x[2], o[0], o[1], *o[2], in_part, out_part, back_part]
    arrays += [gate_up_rows, down_weight, *plane_acts]
    hidden, width = down_weight.shape
    near = x[0].shape[0]
    rows = 16 * near
    vmem = pl.BlockSpec(memory_space=pltpu.VMEM)
    low = [
        (2, hidden, width),
        (hidden, width),
        (2, hidden, width),
        (hidden, width),
        (4, in_part.shape[0] // 4, in_part.shape[1]),
        (4, out_part.shape[0] // 4, width),
        (4, near, width),
        (3, near, width),
        (near, width),
    ]
    got = pl.pallas_call(
        grads_kernel,
        grid=(2,),
        in_specs=anywhere(len(arrays)) + [vmem, vmem],
        out_specs=anywhere(len(low)) + [vmem, vmem, vmem],
        out_shape=[jax.ShapeDtypeStruct(shape, BF16) for shape in low]
        + [
            jax.ShapeDtypeStruct(small.shape, F32),
            jax.ShapeDtypeStruct((8, width), F32),
            jax.ShapeDtypeStruct(init.shape, F32),
        ],
        scratch_shapes=[
            pltpu.VMEM((rows, width), BF16),
            pltpu.VMEM((rows, width), BF16),
            pltpu.VMEM((UNITS, rows), BF16),
            pltpu.VMEM((UNITS, rows), BF16),
            pltpu.VMEM((UNITS, rows), BF16),
            pltpu.VMEM((2, UNITS, width), BF16),
            pltpu.VMEM((UNITS, width), BF16),
            pltpu.VMEM((2, 3, UNITS, SPAN), BF16),
            pltpu.VMEM((4, near, width), BF16),
            pltpu.VMEM((2, near, width), BF16),
            pltpu.VMEM((3, *small.shape), F32),
            pltpu.VMEM((7, 8, width), F32),
            pltpu.VMEM((3, *init.shape), F32),
            *reduce_buffers(in_part),
            *reduce_buffers(out_part),
            pltpu.SemaphoreType.DMA((29,)),
            pltpu.SemaphoreType.DMA((8,)),
            pltpu.SemaphoreType.DMA((8, 6)),
            pltpu.SemaphoreType.DMA((8, 6)),
            pltpu.SemaphoreType.DMA((6, 11)),
            pltpu.SemaphoreType.DMA((6, 11)),
        ],
        compiler_params=pltpu.CompilerParams(
            vmem_limit_bytes=VMEM_MOST, collective_id=collective_id, has_side_effects=True
        ),
        cost_estimate=pl.CostEstimate(
            flops=11 * rows * hidden * width, bytes_accessed=14 * hidden * width, transcendentals=rows * hidden
        ),
        name="mlp_grads",
    )(*arrays, small, init)
    return got[:6], got[7], got[8], got[9], got[10], got[11]


def dots_kernel(*refs):
    dproj, columns, weight, rate, first_gain, mlp_part, dgain, dbias = refs[:8]
    side_a, side_b, in_part, back_part, small, corner_a, corner_b, send, recv = refs[8:]
    step = pl.program_id(0)
    wide = weight.shape[1]
    near = near_peers()[:2]
    moves = [(side_a, corner_a, near[1]), (side_b, corner_b, near[0])]

    @pl.when(step == 0)
    def _():
        greet(near)
        launch(moves, send, recv)

    in_part[...] = mm_tn(columns[...], dproj[:, :wide]).astype(BF16)
    rates = mm_tn(dproj[:, wide:], columns[...])
    back = mm_nt(dproj[:, :wide], weight[...]) + mm(dproj[:, wide:], rate[...])
    back_part[...] = back.astype(BF16)
    gains = jnp.sum(back * columns[...].astype(F32), axis=0, keepdims=True)
    small[...] = jnp.zeros_like(small)
    small[8:16, :] = rates[:8]
    small[0:1, :] = gains / first_gain[...]
    small[1:2, :] = mlp_part[...]

    @pl.when(step == 0)
    def _():
        small[2:3, : dgain.shape[1]] = dgain[...]
        small[2:3, dgain.shape[1] : 2 * dgain.shape[1]] = dbias[...]

    @pl.when(step == pl.num_programs(0) - 1)
    def _():
        settle(moves, send, recv)


def dots(dproj, gathered, weight, rate, gains, mlp_part, dgain, dbias, side_a, side_b, collective_id):
    rows, width = gathered.shape
    full = lambda *shape: pl.BlockSpec(shape, lambda i: (0,) * len(shape))
    cols = lambda height: pl.BlockSpec((height, SPAN), lambda i: (0, i))
    down = lambda wide: pl.BlockSpec((SPAN, wide), lambda i: (i, 0))
    return pl.pallas_call(
        dots_kernel,
        grid=(width // SPAN,),
        in_specs=[
            full(*dproj.shape),
            cols(rows),
            down(weight.shape[1]),
            cols(rate.shape[0]),
            cols(1),
            cols(1),
            full(*dgain.shape),
            full(*dbias.shape),
            *anywhere(2),
        ],
        out_specs=[down(weight.shape[1]), cols(rows), cols(16), *anywhere(2)],
        out_shape=[
            jax.ShapeDtypeStruct(weight.shape, BF16),
            jax.ShapeDtypeStruct((rows, width), BF16),
            jax.ShapeDtypeStruct((16, width), F32),
            *[jax.ShapeDtypeStruct(side_a.shape, BF16)] * 2,
        ],
        scratch_shapes=sem_pair(2),
        compiler_params=pltpu.CompilerParams(
            vmem_limit_bytes=VMEM_MOST, collective_id=collective_id, has_side_effects=True
        ),
        cost_estimate=pl.CostEstimate(
            flops=4 * rows * width * dproj.shape[1], bytes_accessed=24 * 1024 * 1024, transcendentals=0
        ),
        name="dots",
    )(dproj, gathered, weight, rate, gains, mlp_part, dgain, dbias, side_a, side_b)


def finish_kernel(*refs):
    own_gu, far_gu, own_down, far_down, in_ref, out_ref = refs[:6]
    tokens, hidden, d_hidden, gain, plane_total, back_own, back_got = refs[6:13]
    small, sums, init_in = refs[13:16]
    gu, down, in_out, out_out, result, d_tokens = refs[16:22]
    first, second, mix_gain, mix_bias, d_rate, d_init = refs[22:]

    @pl.when(pl.program_id(0) == 0)
    def _():
        local = mix_gain.shape[1]
        first[...] = sums[0:1, :]
        second[...] = sums[1:2, :]
        mix_gain[...] = small[2:3, :local]
        mix_bias[...] = small[2:3, local : 2 * local]
        d_rate[...] = small[8 : 8 + d_rate.shape[0], :]
        d_init[...] = init_in[...]

    gu[...] = own_gu[...].astype(F32) + far_gu[...].astype(F32)
    down[...] = own_down[...].astype(F32) + far_down[...].astype(F32)
    width = in_out.shape[2]
    for part in range(4):
        in_out[:, part, :] = in_ref[:, part * width : (part + 1) * width].astype(F32)
    out_out[...] = out_ref[...].astype(F32)
    d_normed = back_own[...].astype(F32)
    for at in range(3):
        d_normed = d_normed + back_got[at].astype(F32)
    result[...] = (hidden[...] + plane_total[...]).astype(BF16)
    source = tokens[...].astype(F32)
    d_tokens[...] = d_hidden[...] + norm_back(source, rms_scale(source), gain[...], d_normed)


def finish(own_gu, far_gu, own_down, far_down, in_all, out_all, tokens, hidden, d_hidden, gain, plane_total, backs, small, sums, init, local):
    units, width = own_down.shape
    tall, wide = in_all.shape
    near = tokens.shape[0]
    steps = pl.cdiv(units, FINISH)
    rows = lambda *shape: pl.BlockSpec(shape, lambda i: (i,) + (0,) * (len(shape) - 1))
    few = near // steps
    full = lambda *shape: pl.BlockSpec(shape, lambda i: (0,) * len(shape))
    little = [(1, width), (1, width), (1, local), (1, local), (init.shape[0], width), init.shape]
    return pl.pallas_call(
        finish_kernel,
        grid=(steps,),
        in_specs=[tile(2, FINISH, width)] * 2
        + [tile(FINISH, width)] * 2
        + [rows(tall // steps, wide), rows(out_all.shape[0] // steps, width)]
        + [rows(few, width)] * 3
        + [pl.BlockSpec((1, width), lambda i: (0, 0)), rows(few, width)]
        + [rows(few, width), tile(3, few, width)]
        + [full(*small.shape), full(*sums.shape), full(*init.shape)],
        out_specs=[
            tile(2, FINISH, width),
            tile(FINISH, width),
            rows(tall // steps, 4, wide // 4),
            rows(out_all.shape[0] // steps, width),
            rows(few, width),
            rows(few, width),
            *[full(*shape) for shape in little],
        ],
        out_shape=[
            jax.ShapeDtypeStruct((2, units, width), F32),
            jax.ShapeDtypeStruct((units, width), F32),
            jax.ShapeDtypeStruct((tall, 4, wide // 4), F32),
            jax.ShapeDtypeStruct(out_all.shape, F32),
            jax.ShapeDtypeStruct((near, width), BF16),
            jax.ShapeDtypeStruct((near, width), F32),
            *[jax.ShapeDtypeStruct(shape, F32) for shape in little],
        ],
        compiler_params=pltpu.CompilerParams(vmem_limit_bytes=VMEM_MOST),
        cost_estimate=pl.CostEstimate(
            flops=3 * units * width, bytes_accessed=24 * units * width, transcendentals=0
        ),
        name="finish",
    )(own_gu, far_gu, own_down, far_down, in_all, out_all, tokens, hidden, d_hidden, gain, plane_total, *backs, small, sums, init)


PIECE = 2048


def rms_scale(values):
    return lax.rsqrt(jnp.mean(values * values, axis=-1, keepdims=True) + 1e-06)


def norm_back(values, row_scale, gains, upstream):
    weighted = upstream * gains
    return row_scale * weighted - values * row_scale**3 * jnp.mean(
        weighted * values, axis=-1, keepdims=True
    )


def contract_rows(left, right):
    return lax.dot_general(
        left, right, (((0,), (0,)), ((), ())), preferred_element_type=jnp.float32
    )


def contract_cols(left, right):
    return lax.dot_general(
        left, right, (((1,), (1,)), ((), ())), preferred_element_type=jnp.float32
    )


def after(values, *others):
    return lax.optimization_barrier((values, *others))[0]


def swap_core(values):
    size = lax.axis_size("head")
    return lax.ppermute(values, "head", [(at, at ^ 1) for at in range(size)])


def shift_chip(values, hops):
    size = lax.axis_size("head")
    return lax.ppermute(values, "head", [(at, (at + 2 * hops) % size) for at in range(size)])


def swap_mlp(values, flip):
    size = lax.axis_size("mlp")
    return lax.ppermute(values, "mlp", [(at, at ^ flip) for at in range(size)])


def sum_small(values, axis):
    size = lax.axis_size(axis)
    flip = 1
    while flip < size:
        values = values + lax.ppermute(values, axis, [(at, at ^ flip) for at in range(size)])
        flip *= 2
    return values


def spread_mlp(values):
    return [values] + [swap_mlp(values, flip) for flip in range(1, lax.axis_size("mlp"))]


def scatter_mlp(parts):
    total = parts[0]
    for flip in range(1, len(parts)):
        total = total + swap_mlp(parts[flip].astype(BF16), flip).astype(F32)
    return total


def sum_mlp(values, shape):
    size = lax.axis_size("mlp")
    me = lax.axis_index("mlp")
    rows = values.shape[0] // size
    low = values.astype(BF16)
    total = lax.dynamic_slice_in_dim(values, me * rows, rows)
    for flip in range(1, size):
        part = lax.dynamic_slice_in_dim(low, (me ^ flip) * rows, rows)
        total = total + swap_mlp(part, flip).astype(F32)
    own = total.astype(BF16)
    whole = jnp.zeros((values.shape[0],) + shape, F32)
    start = (0,) * len(shape)
    whole = lax.dynamic_update_slice(whole, total.reshape((rows,) + shape), (me * rows,) + start)
    for flip in range(1, size):
        part = swap_mlp(own, flip).astype(F32).reshape((rows,) + shape)
        whole = lax.dynamic_update_slice(whole, part, ((me ^ flip) * rows,) + start)
    return whole


def on_device(
    tokens,
    out_grad,
    seq_lengths,
    norm_gain,
    in_weight,
    rate_weight,
    init_state,
    mix_gain,
    mix_bias,
    out_weight,
    mlp_gain,
    gate_up,
    down_weight,
):
    core = lax.axis_index("head") % 2
    chips = lax.axis_size("head") // 2
    row_total = tokens.shape[1]
    model_width = tokens.shape[2]
    local_width = in_weight.shape[2]
    head_count = init_state.shape[0]
    first_gain = norm_gain.astype(jnp.float32)
    second_gain = mlp_gain.astype(jnp.float32)
    source = tokens[0].astype(jnp.float32)
    cotangent = out_grad[0]
    first_scale = rms_scale(source)
    normed = (source * first_scale * first_gain).astype(BF16)
    gathered = lax.all_gather(normed, "head", axis=0, tiled=True)
    in_flat = jnp.concatenate(
        [
            in_weight.reshape(model_width, 4 * local_width),
            rate_weight,
            jnp.zeros((model_width, LANES - head_count), BF16),
        ],
        axis=1,
    )
    cot_plane = spread_mlp(cotangent)
    projected = jnp.dot(gathered, in_flat, preferred_element_type=jnp.float32)
    mix_gains = mix_gain.astype(jnp.float32)[None]
    mix_biases = mix_bias.astype(jnp.float32)[None]
    (mixed, *kept), _ = mixer_forward(
        seq_lengths, projected, init_state, mix_gains, mix_biases, Carry()
    )

    late_out_weight, late_cotangent, _ = lax.optimization_barrier((out_weight, cotangent, gathered))
    out_full = lax.all_gather(late_out_weight, "head", axis=0, tiled=True)
    cot_far = [shift_chip(late_cotangent, hops) for hops in range(1, chips)]
    cot_far = jnp.concatenate(cot_far, axis=0)
    cot_all = jnp.concatenate(cot_plane + spread_mlp(cot_far), axis=0)
    cot_plane = jnp.concatenate(cot_plane, axis=0)

    mixed_rows = lax.all_to_all(mixed, "head", 0, 1, tiled=True)
    branch = jnp.dot(mixed_rows, out_full, preferred_element_type=jnp.float32)
    hidden = source + branch
    second_scale = rms_scale(hidden)
    normed2 = (hidden * second_scale * second_gain).astype(BF16)

    gate_up_rows = jnp.transpose(gate_up, (1, 2, 0))
    gate_rows, up_rows = gate_up_rows[0], gate_up_rows[1]
    normed_plane = spread_mlp(normed2)
    normed_far = [shift_chip(normed2, hops) for hops in range(1, chips)]
    plane = jnp.concatenate(normed_plane, axis=0)
    gate = contract_cols(plane, gate_rows)
    up = contract_cols(plane, up_rows)
    silu, slope = gated(gate, up)
    d_act = contract_cols(cot_plane, down_weight)
    d_gate = (d_act * up * slope).astype(BF16)
    d_up = (d_act * silu).astype(BF16)
    d_plane = jnp.dot(d_gate, gate_rows, preferred_element_type=jnp.float32) + jnp.dot(
        d_up, up_rows, preferred_element_type=jnp.float32
    )
    members = lax.axis_size("mlp")
    d_normed2 = scatter_mlp([d_plane[at * row_total : (at + 1) * row_total] for at in range(members)])
    activation = (silu * up).astype(BF16)
    out_plane = jnp.dot(activation, down_weight, preferred_element_type=jnp.float32)
    mlp_out = scatter_mlp([out_plane[at * row_total : (at + 1) * row_total] for at in range(members)])
    result = (hidden + mlp_out).astype(BF16)[None]

    grad_mlp_gain = sum_small(
        sum_small(jnp.sum(d_normed2 * hidden * second_scale, axis=0), "mlp"), "head"
    )
    d_hidden = cotangent.astype(jnp.float32) + norm_back(
        hidden, second_scale, second_gain, d_normed2
    )
    d_branch = d_hidden.astype(BF16)
    d_mixed_rows = contract_cols(d_branch, out_full).astype(BF16)
    d_mixed = lax.all_to_all(d_mixed_rows, "head", 1, 0, tiled=True)
    shard_rows = lax.all_gather(d_branch, "head", axis=0, tiled=True)
    (d_projected, grad_init_state, grad_mix_gain, grad_mix_bias), _ = mixer_backward(
        seq_lengths, d_mixed, projected, init_state, mix_gains, mix_biases, kept, Carry()
    )
    grad_in_flat = contract_rows(gathered, d_projected)
    grad_in_weight = sum_mlp(grad_in_flat[:, : 4 * local_width], (4, local_width))
    d_normed = lax.psum_scatter(
        contract_cols(d_projected, in_flat).astype(BF16),
        "head",
        scatter_dimension=0,
        tiled=True,
    ).astype(jnp.float32)
    grad_out_weight = sum_mlp(contract_rows(mixed, shard_rows), (model_width,))
    small = jnp.concatenate(
        [
            grad_in_flat[:, 4 * local_width : 4 * local_width + head_count].reshape(-1),
            grad_init_state.reshape(-1),
            grad_mix_gain[0],
            grad_mix_bias[0],
        ]
    )
    small = sum_small(small, "mlp")
    sizes = [model_width * head_count, grad_init_state.size, local_width, local_width]
    ends = [sum(sizes[: at + 1]) for at in range(4)]
    grad_rate_weight = small[: ends[0]].reshape(model_width, head_count)
    grad_init_state = small[ends[0] : ends[1]].reshape(grad_init_state.shape)
    grad_mix_gain = small[ends[1] : ends[2]]
    grad_mix_bias = small[ends[2] : ends[3]]
    grad_norm_gain = sum_small(
        sum_small(jnp.sum(d_normed * source * first_scale, axis=0), "mlp"), "head"
    )
    grad_tokens = d_hidden + norm_back(source, first_scale, first_gain, d_normed)

    far, _ = lax.optimization_barrier((jnp.concatenate(normed_far, axis=0), d_normed2))
    normed_all = jnp.concatenate(normed_plane + spread_mlp(far), axis=0)
    half = model_width // 2
    pieces = max(1, normed_all.shape[0] // PIECE)
    piece = normed_all.shape[0] // pieces
    sums = None
    for at in range(pieces):
        rows_in = normed_all[at * piece : (at + 1) * piece]
        rows_cot = cot_all[at * piece : (at + 1) * piece]
        if sums is not None:
            rows_in, rows_cot, sums = lax.optimization_barrier((rows_in, rows_cot, sums))
        gate = contract_cols(rows_in, gate_rows)
        up = contract_cols(rows_in, up_rows)
        silu, slope = gated(gate, up)
        activation = (silu * up).astype(BF16)
        d_act = contract_cols(rows_cot, down_weight)
        d_gate = d_act * up * slope
        d_up = d_act * silu
        mine = jnp.where(core == 0, d_gate, d_up).astype(BF16)
        theirs = jnp.where(core == 0, d_up, d_gate).astype(BF16)
        cot_theirs = jnp.where(core == 0, rows_cot[:, half:], rows_cot[:, :half])
        cot_mine = jnp.where(core == 0, rows_cot[:, :half], rows_cot[:, half:])
        terms = [
            contract_rows(theirs, rows_in),
            contract_rows(activation, cot_theirs),
            contract_rows(mine, rows_in),
            contract_rows(activation, cot_mine),
        ]
        sums = terms if sums is None else [old + new for old, new in zip(sums, terms)]
    gate_theirs = swap_core(sums[0].astype(BF16))
    down_theirs = swap_core(sums[1].astype(BF16))
    gate_mine = sums[2] + gate_theirs.astype(F32)
    down_mine = sums[3] + down_theirs.astype(F32)
    gate_other = swap_core(gate_mine.astype(BF16)).astype(F32)
    down_other = swap_core(down_mine.astype(BF16)).astype(F32)
    grad_gate_up = jnp.stack(
        [jnp.where(core == 0, gate_mine, gate_other), jnp.where(core == 0, gate_other, gate_mine)]
    )
    grad_gate_up = jnp.transpose(grad_gate_up, (2, 0, 1))
    grad_down = jnp.concatenate(
        [jnp.where(core == 0, down_mine, down_other), jnp.where(core == 0, down_other, down_mine)],
        axis=1,
    )
    return (
        result,
        grad_tokens[None],
        grad_norm_gain,
        grad_in_weight,
        grad_rate_weight,
        grad_init_state,
        grad_mix_gain,
        grad_mix_bias,
        grad_out_weight,
        grad_mlp_gain,
        grad_gate_up,
        grad_down,
    )


def spread_kernel(*refs):
    mixed_rows, tokens, gain, out_cross, out_other, cot, cot_line = refs[:7]
    hidden, normed2, got, line, side_x, side_y = refs[7:13]
    weights, loads, send, recv = refs[13:]
    across, along = near_peers()[:2]
    half = tokens.shape[0] // 2
    top, bottom = pl.ds(0, half), pl.ds(half, half)
    direct = [(normed2, got.at[0], across), (normed2, got.at[1], along)]
    corner = [
        (got.at[0, top], got.at[2, top], along),
        (got.at[1, bottom], got.at[2, bottom], across),
    ]
    rest = line_moves(cot, 1, line) + [(cot_line, side_x, across), (cot_line, side_y, along)]
    fetch = [
        pltpu.make_async_copy(part, weights.at[at], loads.at[at])
        for at, part in enumerate((out_cross, out_other))
    ]
    for copy in fetch:
        copy.start()
    greet([across, along, *line_peers()])
    launch(rest, send.at[2], recv.at[2])
    for copy in fetch:
        copy.wait()

    def body(at, _):
        span = pl.ds(pl.multiple_of(at * SPAN, SPAN), SPAN)
        branch = mm(mixed_rows[0], weights[0, :, span]) + mm(mixed_rows[1], weights[1, :, span])
        hidden[:, span] = tokens[:, span].astype(F32) + branch
        return 0

    lax.fori_loop(0, tokens.shape[1] // SPAN, body, 0)
    values = hidden[...]
    normed2[...] = (values * rms_scale(values) * gain[:, values.shape[1] : 2 * values.shape[1]]).astype(BF16)
    launch(direct, send.at[0], recv.at[0])
    settle(direct, send.at[0], recv.at[0])
    launch(corner, send.at[1], recv.at[1])
    settle(corner, send.at[1], recv.at[1])
    settle(rest, send.at[2], recv.at[2])


def spread_plane(mixed_rows, tokens, gains, out_halves, cot, cot_line, collective_id):
    rows, width = tokens.shape
    vmem = pl.BlockSpec(memory_space=pltpu.VMEM)
    return pl.pallas_call(
        spread_kernel,
        in_specs=[vmem, vmem, vmem, *anywhere(4)],
        out_specs=[vmem, vmem, *anywhere(4)],
        out_shape=[
            jax.ShapeDtypeStruct((rows, width), F32),
            jax.ShapeDtypeStruct((rows, width), BF16),
            jax.ShapeDtypeStruct((3, rows, width), BF16),
            *[jax.ShapeDtypeStruct((3 * rows // 2, width), BF16)] * 3,
        ],
        scratch_shapes=[
            pltpu.VMEM((2, width // 2, width), BF16),
            pltpu.SemaphoreType.DMA((2,)),
            pltpu.SemaphoreType.DMA((3, 5)),
            pltpu.SemaphoreType.DMA((3, 5)),
        ],
        compiler_params=pltpu.CompilerParams(
            vmem_limit_bytes=VMEM_MOST, collective_id=collective_id, has_side_effects=True
        ),
        cost_estimate=pl.CostEstimate(
            flops=2 * rows * width * width, bytes_accessed=3 * width * width, transcendentals=0
        ),
        name="spread_plane",
    )(mixed_rows, tokens, gains, *out_halves, cot, cot_line)


class PlaneSum:
    def __init__(self, parts, bufs, send, recv, loads):
        self.parts = parts
        self.got, self.own, self.passed, self.kept, self.late = bufs
        self.send, self.recv, self.loads = send, recv, loads
        self.across, self.along = near_peers()[:2]
        half = parts.shape[1] // 2
        self.spans = (pl.ds(0, half), pl.ds(half, half))

    def moves(self, phase):
        top, bottom = self.spans
        if phase == 0:
            return [
                (self.parts.at[1, top], self.got.at[0], self.across),
                (self.parts.at[3, top], self.got.at[1], self.across),
                (self.parts.at[2, bottom], self.got.at[2], self.along),
                (self.parts.at[3, bottom], self.got.at[3], self.along),
            ]
        return [
            (self.passed.at[0], self.late.at[0], self.along),
            (self.passed.at[1], self.late.at[1], self.across),
        ]

    def begin(self):
        launch(self.moves(0), self.send.at[0], self.recv.at[0])

    def middle(self):
        top, bottom = self.spans
        gather_parts(
            [
                (self.parts.at[0, top], self.own.at[0]),
                (self.parts.at[2, top], self.own.at[1]),
                (self.parts.at[0, bottom], self.own.at[2]),
                (self.parts.at[1, bottom], self.own.at[3]),
            ],
            self.loads,
        )
        settle(self.moves(0), self.send.at[0], self.recv.at[0])
        for half in range(2):
            self.passed[half] = (
                self.own[2 * half + 1].astype(F32) + self.got[2 * half + 1].astype(F32)
            ).astype(BF16)
        launch(self.moves(1), self.send.at[1], self.recv.at[1])
        for half in range(2):
            self.kept[half] = self.own[2 * half].astype(F32) + self.got[2 * half].astype(F32)

    def finish(self, target):
        settle(self.moves(1), self.send.at[1], self.recv.at[1])
        for half in range(2):
            target[self.spans[half], :] = self.kept[half] + self.late[half].astype(F32)


def plane_buffers(rows, width):
    half = rows // 2
    return [
        pltpu.VMEM((4, half, width), BF16),
        pltpu.VMEM((4, half, width), BF16),
        pltpu.VMEM((2, half, width), BF16),
        pltpu.VMEM((2, half, width), F32),
        pltpu.VMEM((2, half, width), BF16),
    ]


def turn_kernel(*refs):
    d_plane, out_plane, normed2, out_cross, out_other, hidden, cot, gain = refs[:8]
    d_mixed, line, d_hidden, d_branch, mlp_part, plane_total = refs[8:14]
    d_bufs, out_bufs, weights, slots, d_normed = refs[14:19], refs[19:24], refs[24], refs[25], refs[26]
    sum_send, sum_recv, loads, row_send, row_recv, line_send, line_recv = refs[27:]
    me = lax.axis_index("head")
    chip, core = me // 2, lax.rem(me, 2)
    rows = hidden.shape[0]
    width = slots.shape[2]
    d_sum = PlaneSum(d_plane, d_bufs, sum_send.at[0], sum_recv.at[0], loads)
    out_sum = PlaneSum(out_plane, out_bufs, sum_send.at[1], sum_recv.at[1], loads)
    line_copies = line_moves(normed2, 1, line)
    fetch = [
        pltpu.make_async_copy(part, weights.at[at], loads.at[4 + at])
        for at, part in enumerate((out_cross, out_other))
    ]
    greet([d_sum.across, d_sum.along] + [head_peer(at) for at in range(1, 8)])
    d_sum.begin()
    launch(line_copies, line_send, line_recv)
    for copy in fetch:
        copy.start()
    d_sum.middle()
    d_sum.finish(d_normed)
    out_sum.begin()
    scale = rms_scale(hidden[...])
    part = d_normed[...]
    mlp_part[...] = jnp.sum(part * hidden[...] * scale, axis=0, keepdims=True)
    gains = gain[:, part.shape[1] : 2 * part.shape[1]]
    total = cot[...].astype(F32) + norm_back(hidden[...], scale, gains, part)
    d_hidden[...] = total
    d_branch[...] = total.astype(BF16)
    for copy in fetch:
        copy.wait()

    def row_copy(at, ahead, sender, target, local):
        place = d_mixed.at[pl.ds(pl.multiple_of(me * rows, rows), rows)]
        if local:
            return pltpu.make_async_copy(slots.at[at], place, row_send.at[at])
        return pltpu.make_async_remote_copy(
            src_ref=slots.at[at],
            dst_ref=place,
            send_sem=row_send.at[at],
            recv_sem=row_recv.at[ahead],
            device_id={"head": target},
            device_id_type=MESH,
        )

    order = (4, 3, 5, 2, 6, 1, 7, 0)
    for at, ahead in enumerate(order):
        target = lax.rem(me + ahead, 8)
        columns = pl.ds(pl.multiple_of(target // 2 * width, width), width)
        slots[at] = mm_nt(d_branch[...], weights[ahead % 2, columns, :]).astype(BF16)
        row_copy(at, ahead, me, target, ahead == 0).start()
    out_sum.middle()
    for at, ahead in enumerate(order):
        copy = row_copy(at, ahead, me, lax.rem(me + ahead, 8), ahead == 0)
        copy.wait()
    out_sum.finish(plane_total)
    settle(line_copies, line_send, line_recv)


def turn(d_plane, out_plane, normed2, out_halves, hidden, cot, gains, local_width, collective_id):
    rows, width = normed2.shape
    vmem = pl.BlockSpec(memory_space=pltpu.VMEM)
    return pl.pallas_call(
        turn_kernel,
        in_specs=anywhere(5) + [vmem] * 3,
        out_specs=anywhere(2) + [vmem] * 4,
        out_shape=[
            jax.ShapeDtypeStruct((8 * rows, local_width), BF16),
            jax.ShapeDtypeStruct((3 * rows // 2, width), BF16),
            jax.ShapeDtypeStruct((rows, width), F32),
            jax.ShapeDtypeStruct((rows, width), BF16),
            jax.ShapeDtypeStruct((1, width), F32),
            jax.ShapeDtypeStruct((rows, width), F32),
        ],
        scratch_shapes=[
            *plane_buffers(rows, width),
            *plane_buffers(rows, width),
            pltpu.VMEM((2, width // 2, width), BF16),
            pltpu.VMEM((8, rows, local_width), BF16),
            pltpu.VMEM((rows, width), F32),
            pltpu.SemaphoreType.DMA((2, 2, 4)),
            pltpu.SemaphoreType.DMA((2, 2, 4)),
            pltpu.SemaphoreType.DMA((6,)),
            *sem_pair(8),
            *sem_pair(3),
        ],
        compiler_params=pltpu.CompilerParams(
            vmem_limit_bytes=VMEM_MOST, collective_id=collective_id, has_side_effects=True
        ),
        cost_estimate=pl.CostEstimate(
            flops=2 * rows * width * width, bytes_accessed=4 * width * width, transcendentals=0
        ),
        name="turn",
    )(d_plane, out_plane, normed2, *out_halves, hidden, cot, gains)


def halves_of(values):
    half = values.shape[0] // 2
    return pl.ds(0, half), pl.ds(half, half)


def sides_and_line(ins, outs):
    across, along = near_peers()[:2]
    top, bottom = halves_of(outs[2])
    moves = [
        (ins[0], outs[0], across),
        (ins[0], outs[1], along),
        (ins[1].at[top], outs[2].at[top], along),
        (ins[2].at[bottom], outs[2].at[bottom], across),
    ]
    return [across, along, *line_peers()], moves + line_moves(ins[3], 0, outs[4])


def corner_rest(ins, outs):
    across, along = near_peers()[:2]
    top, bottom = halves_of(outs[3])
    return [
        (outs[0].at[top], outs[3].at[top], along),
        (outs[1].at[bottom], outs[3].at[bottom], across),
    ]


def sides(ins, outs):
    near = near_peers()[:2]
    return near, [(ins[at // 2], outs[at], near[at % 2]) for at in range(4)]


def on_square(
    tokens,
    out_grad,
    seq_lengths,
    norm_gain,
    in_weight,
    rate_weight,
    init_state,
    mix_gain,
    mix_bias,
    out_weight,
    mlp_gain,
    gate_up,
    down_weight,
):
    heads = lax.axis_size("head")
    rows = tokens.shape[1]
    model_width = tokens.shape[2]
    local_width = in_weight.shape[2]
    head_count = init_state.shape[0]
    vectors = [part.reshape(-1, LANES) for part in (norm_gain, mlp_gain, mix_gain, mix_bias)]
    source = tokens[0]
    cotangent = out_grad[0]
    far_shape = (3 * rows // 2, model_width)
    (projected, rate_rows), (mixed, *kept), gains, moved = head(
        seq_lengths, source, rate_weight.T, init_state, vectors, in_weight, cotangent, out_weight, 0
    )
    gathered, cot_got, in_main, mixed_rows, out_cross, out_other, cot_line_a = moved
    out_halves = [part.reshape(model_width // 2, model_width) for part in (out_cross, out_other)]
    hidden, normed2, normed_got, cot_line_b, cot_x_a, cot_y_a = spread_plane(
        mixed_rows, source, gains, out_halves, cotangent, cot_line_a, 3
    )
    gate_up_rows = jnp.transpose(gate_up, (1, 2, 0))
    (d_plane, out_plane), plane_acts, moved = mlp_plane(
        normed2,
        normed_got,
        cotangent,
        cot_got,
        gate_up_rows,
        down_weight,
        Carry(
            [cot_line_b, cot_x_a, cot_y_a, normed2],
            [far_shape] * 5,
            sides_and_line,
            9,
            4,
            (1, 2, corner_rest),
        ),
    )
    cot_x_b, cot_y_b, cot_corner_a, cot_corner_b, normed_line_a = moved
    d_mixed, normed_line_b, d_hidden, d_branch, mlp_part, plane_total = turn(
        d_plane,
        out_plane,
        normed2,
        out_halves,
        hidden,
        cotangent,
        gains,
        local_width,
        5,
    )
    shard_rows = lax.all_gather(after(d_branch, d_mixed), "head", axis=0, tiled=True)
    (d_projected, grad_init_state, grad_mix_gain, grad_mix_bias), normed_sides = mixer_backward(
        seq_lengths,
        d_mixed,
        projected,
        init_state,
        gains,
        gains,
        kept,
        Carry([normed_line_a, normed_line_b], [far_shape] * 4, sides, 4, 7),
        (2 * model_width // local_width, 2 * model_width // local_width + 1),
    )
    in_part, back_part, small, normed_corner_a, normed_corner_b = dots(
        d_projected,
        gathered,
        in_main,
        rate_rows,
        gains,
        mlp_part,
        grad_mix_gain,
        grad_mix_bias,
        normed_sides[0],
        normed_sides[3],
        8,
    )
    out_part = contract_rows(mixed, after(shard_rows, in_part)).astype(BF16)
    cot_far = [cot_line_a, cot_line_b, cot_x_a, cot_x_b, cot_y_a, cot_y_b]
    normed_far = [normed_line_a, normed_line_b]
    normed_far += [normed_sides[0], normed_sides[2], normed_sides[1], normed_sides[3]]
    grads, back_got, back_own, small, sums, grad_init_state = mlp_grads(
        (normed2, normed_got, [*normed_far, normed_corner_a, normed_corner_b]),
        (cotangent, cot_got, [*cot_far, cot_corner_a, cot_corner_b]),
        in_part,
        out_part,
        back_part.reshape(heads // 2, 2, rows, model_width),
        gate_up_rows,
        down_weight,
        plane_acts,
        small,
        grad_init_state,
        9,
    )
    own_gate_up, own_down, other_gate_up, other_down, in_all, out_all = grads
    done = finish(
        own_gate_up,
        other_gate_up,
        own_down,
        other_down,
        in_all.reshape(in_main.shape),
        out_all.reshape(out_weight.shape),
        tokens[0],
        hidden,
        d_hidden,
        gains,
        plane_total,
        (back_own, back_got),
        small,
        sums,
        grad_init_state,
        local_width,
    )
    grad_gate_up, grad_down, grad_in_weight, grad_out_weight, result, grad_tokens = done[:6]
    grad_norm_gain, grad_mlp_gain, grad_mix_gain, grad_mix_bias, grad_rate, grad_init_state = done[6:]
    grad_gate_up = jnp.transpose(grad_gate_up, (2, 0, 1))
    return (
        result[None],
        grad_tokens[None],
        grad_norm_gain[0],
        grad_in_weight,
        grad_rate.T,
        grad_init_state,
        grad_mix_gain[0],
        grad_mix_bias[0],
        grad_out_weight,
        grad_mlp_gain[0],
        grad_gate_up,
        grad_down,
    )


def solution(mesh):
    square = mesh.shape["mlp"] == 4 and mesh.shape["head"] == 8
    return jax.shard_map(
        on_square if square else on_device,
        mesh=mesh,
        in_specs=(
            P("mlp", "head", None),
            P("mlp", "head", None),
            P("mlp", None),
            P(),
            P(None, None, "head"),
            P(None, "head"),
            P("head", None, None),
            P("head"),
            P("head"),
            P("head", None),
            P(),
            P(None, None, "mlp"),
            P("mlp", None),
        ),
        out_specs=(
            P("mlp", "head", None),
            P("mlp", "head", None),
            P(),
            P(None, None, "head"),
            P(None, "head"),
            P("head", None, None),
            P("head"),
            P("head"),
            P("head", None),
            P(),
            P(None, None, "mlp"),
            P("mlp", None),
        ),
        check_vma=False,
    )
```

```python
import jax
import jax.numpy as jnp
from jax import lax
from jax.experimental import pallas as pl
from jax.experimental.pallas import tpu as pltpu
from jax.sharding import PartitionSpec as P

HEAD_DIM = 64
MINIBATCH = 16
CHUNK = 128
LANES = 128
VMEM_MOST = 62 * 1024 * 1024
PAIR = LANES // HEAD_DIM
F32 = jnp.float32
BF16 = jnp.bfloat16


def mm(left, right):
    return jnp.dot(left.astype(BF16), right.astype(BF16), preferred_element_type=F32)


def mm_nt(left, right):
    return lax.dot_general(
        left.astype(BF16), right.astype(BF16), (((1,), (1,)), ((), ())), preferred_element_type=F32
    )


def mm_tn(left, right):
    return lax.dot_general(
        left.astype(BF16), right.astype(BF16), (((0,), (0,)), ((), ())), preferred_element_type=F32
    )


def mm_split(left, right):
    high = left.astype(BF16)
    rest = (left - high.astype(F32)).astype(BF16)
    return mm(high, right) + mm(rest, right)


def chunk_masks(len_ref, chunk):
    steps = CHUNK // MINIBATCH
    base = chunk * steps
    row = lax.broadcasted_iota(jnp.int32, (CHUNK, CHUNK), 0)
    col = lax.broadcasted_iota(jnp.int32, (CHUNK, CHUNK), 1)
    row_step = row // MINIBATCH
    col_step = col // MINIBATCH
    row_seq = jnp.zeros((CHUNK, CHUNK), jnp.int32)
    col_seq = jnp.zeros((CHUNK, CHUNK), jnp.int32)
    before = jnp.int32(0)
    last = jnp.int32(0)
    start = jnp.int32(0)
    for at in range(len_ref.shape[1]):
        edge = start - base
        row_seq += (row_step >= edge).astype(jnp.int32)
        col_seq += (col_step >= edge).astype(jnp.int32)
        before += (edge <= -1).astype(jnp.int32)
        last += (edge <= steps - 1).astype(jnp.int32)
        start = start + len_ref[0, at]
    same = row_seq == col_seq
    earlier = jnp.where(same & (col_step < row_step), 1.0, 0.0).astype(F32)
    causal = jnp.where(same & (col <= row), 1.0, 0.0).astype(F32)
    carried = jnp.where(row_seq == before, 1.0, 0.0).astype(F32)
    final = jnp.where(row_seq == last, 1.0, 0.0).astype(F32)
    keep = jnp.where(before == last, 1.0, 0.0).astype(F32)
    return earlier, causal, carried, final, keep


def half_masks():
    lane = lax.broadcasted_iota(jnp.int32, (CHUNK, LANES), 1)
    return [jnp.where(lane // HEAD_DIM == at, 1.0, 0.0).astype(BF16) for at in range(PAIR)]


def same_head(dtype):
    row = lax.broadcasted_iota(jnp.int32, (LANES, LANES), 0) // HEAD_DIM
    col = lax.broadcasted_iota(jnp.int32, (LANES, LANES), 1) // HEAD_DIM
    return jnp.where(row == col, 1.0, 0.0).astype(dtype)


def spread_pair(first, second):
    zero = jnp.zeros((HEAD_DIM, HEAD_DIM), F32)
    return jnp.concatenate(
        [
            jnp.concatenate([first, zero], axis=1),
            jnp.concatenate([zero, second], axis=1),
        ],
        axis=0,
    )


def rates_of(proj_ref, width):
    return jax.nn.sigmoid(proj_ref[:, 4 * width : 4 * width + LANES])


def spread_rate(rates, pair):
    lane = lax.broadcasted_iota(jnp.int32, (CHUNK, LANES), 1)
    first = rates[:, PAIR * pair : PAIR * pair + 1]
    second = rates[:, PAIR * pair + 1 : PAIR * pair + 2]
    return jnp.where(lane < HEAD_DIM, first, second) * (1.0 / (MINIBATCH * HEAD_DIM))


GELU_A = 0.7978845608028654
GELU_B = 0.044715


def gelu_parts(x):
    square = x * x
    bend = jnp.tanh(GELU_A * x * (1.0 + GELU_B * square))
    half = 0.5 * (1.0 + bend)
    slope = half + 0.5 * x * (1.0 - bend * bend) * GELU_A * (1.0 + 3.0 * GELU_B * square)
    return x * half, slope


def scaled_parts(proj_ref, pair, width, rates):
    def part(at):
        return proj_ref[:, at * width + pair * LANES : at * width + (pair + 1) * LANES]

    query = part(0).astype(BF16)
    key = part(1).astype(BF16)
    scaled_key = (key.astype(F32) * spread_rate(rates, pair)).astype(BF16)
    return query, key, scaled_key, part


def forward_local(len_ref, proj_ref, t_ref, a_ref, chunk):
    heads = t_ref.shape[1]
    width = heads * HEAD_DIM
    earlier, causal, _, _, _ = chunk_masks(len_ref, chunk)
    halves = half_masks()
    rates = rates_of(proj_ref, width)
    for pair in range(heads // PAIR):
        query, key, scaled_key, _ = scaled_parts(proj_ref, pair, width, rates)
        for at in range(PAIR):
            head = PAIR * pair + at
            one = -earlier * mm_nt(key * halves[at], scaled_key)
            a_ref[0, head] = (causal * mm_nt(query * halves[at], scaled_key)).astype(BF16)
            one_low = one.astype(BF16)
            two = mm(one_low, one_low)
            two_low = two.astype(BF16)
            total = one + two + mm(two_low, one_low)
            four = mm(two_low, two_low)
            t_ref[0, head] = (total + four + mm(four, total)).astype(BF16)


def forward_state(len_ref, proj_ref, init_ref, e_ref, z_ref, s_ref, t_ref, a_ref, state, first, chunk):
    pairs = state.shape[0]
    width = pairs * LANES

    @pl.when(chunk == 0)
    def _():
        for pair in range(pairs):
            spread = spread_pair(
                init_ref[PAIR * pair].astype(F32), init_ref[PAIR * pair + 1].astype(F32)
            )
            first[pair] = spread
            state[pair] = spread

    _, _, carried, final, keep = chunk_masks(len_ref, chunk)
    halves = half_masks()
    block = same_head(F32)
    rates = rates_of(proj_ref, width)
    outs = []
    for pair in range(pairs):
        lanes = slice(pair * LANES, (pair + 1) * LANES)
        query, key, scaled_key, part = scaled_parts(proj_ref, pair, width, rates)
        value = part(2).astype(BF16).astype(F32)
        now = state[pair]
        start = first[pair]
        both = jnp.concatenate([now, start], axis=1).astype(BF16)
        s_ref[0, pair] = now.astype(BF16)
        key_state = mm(key, both)
        query_state = mm(query, both)
        target = jnp.where(carried > 0.5, key_state[:, :LANES], key_state[:, LANES:]) - value
        target_low = target.astype(BF16)
        error = target
        for at in range(PAIR):
            error = error + mm(t_ref[0, PAIR * pair + at], target_low * halves[at])
        error_low = error.astype(BF16)
        e_ref[:, lanes] = error_low
        state[pair] = (
            keep * now + (1.0 - keep) * start - block * mm_tn(scaled_key * final.astype(BF16), error_low)
        )
        out = jnp.where(carried > 0.5, query_state[:, :LANES], query_state[:, LANES:])
        for at in range(PAIR):
            out = out - mm(a_ref[0, PAIR * pair + at], error_low * halves[at])
        z_ref[:, lanes] = out
        outs.append(out)
    return outs


def forward_tail(outs, gates, gain_ref, bias_ref, mixed_ref):
    mean = same_head(BF16) * (1.0 / HEAD_DIM)
    for pair, out in enumerate(outs):
        lanes = slice(pair * LANES, (pair + 1) * LANES)
        centered = out - mm_split(out, mean)
        normed = centered * lax.rsqrt(mm_split(centered * centered, mean) + 1e-06)
        gelu, _ = gelu_parts(gates[:, lanes])
        mixed_ref[:, lanes] = ((normed * gain_ref[:, lanes] + bias_ref[:, lanes]) * gelu).astype(BF16)


def forward_kernel(len_ref, proj_ref, init_ref, gain_ref, bias_ref, mixed_ref, e_ref, z_ref, s_ref, t_ref, a_ref, state, first):
    chunk = pl.program_id(0)
    width = mixed_ref.shape[1]
    forward_local(len_ref, proj_ref, t_ref, a_ref, chunk)
    outs = forward_state(
        len_ref, proj_ref, init_ref, e_ref, z_ref, s_ref, t_ref, a_ref, state, first, chunk
    )
    forward_tail(outs, proj_ref[:, 3 * width : 4 * width], gain_ref, bias_ref, mixed_ref)


def backward_kernel(
    len_ref, dm_ref, proj_ref, init_ref, gain_ref, bias_ref, e_ref, z_ref, s_ref, t_ref, a_ref,
    dproj_ref, dinit_ref, dgain_ref, dbias_ref, grad, first, dfirst,
):
    step = pl.program_id(0)
    chunks = pl.num_programs(0)
    chunk = chunks - 1 - step
    pairs = grad.shape[0]
    width = pairs * LANES

    @pl.when(step == 0)
    def _():
        for pair in range(pairs):
            first[pair] = spread_pair(
                init_ref[PAIR * pair].astype(F32), init_ref[PAIR * pair + 1].astype(F32)
            ).astype(BF16)
        grad[...] = jnp.zeros_like(grad)
        dfirst[...] = jnp.zeros_like(dfirst)
        dgain_ref[...] = jnp.zeros_like(dgain_ref)
        dbias_ref[...] = jnp.zeros_like(dbias_ref)

    earlier, causal, carried, final, keep = chunk_masks(len_ref, chunk)
    halves = half_masks()
    block = same_head(F32)
    mean = same_head(BF16) * (1.0 / HEAD_DIM)
    rates = rates_of(proj_ref, width)
    drate = jnp.zeros((CHUNK, LANES), F32)
    for pair in range(pairs):
        lanes = slice(pair * LANES, (pair + 1) * LANES)

        def spot(at):
            return slice(at * width + pair * LANES, at * width + (pair + 1) * LANES)

        query = proj_ref[:, spot(0)].astype(BF16)
        key = proj_ref[:, spot(1)].astype(BF16)
        gate = proj_ref[:, spot(3)]
        rate = spread_rate(rates, pair)
        key_wide = key.astype(F32)
        scaled_key = (key_wide * rate).astype(BF16)
        out = z_ref[:, lanes]
        centered = out - mm_split(out, mean)
        scale = lax.rsqrt(mm_split(centered * centered, mean) + 1e-06)
        normed = centered * scale
        gain = gain_ref[:, lanes]
        gelu, slope = gelu_parts(gate)
        dmixed = dm_ref[:, lanes].astype(F32)
        dy = dmixed * gelu
        dproj_ref[:, spot(3)] = (dmixed * (normed * gain + bias_ref[:, lanes]) * slope).astype(BF16)
        dgain_ref[:, lanes] += jnp.sum(dy * normed, axis=0, keepdims=True)
        dbias_ref[:, lanes] += jnp.sum(dy, axis=0, keepdims=True)
        dnormed = dy * gain
        dout = scale * (dnormed - mm_split(dnormed, mean) - normed * mm_split(dnormed * normed, mean))
        dout_low = dout.astype(BF16)
        error = e_ref[:, lanes]
        upper = grad[pair]
        upper_low = upper.astype(BF16)
        derror = -rate * final * mm(key, upper_low)
        for at in range(PAIR):
            derror = derror - mm_tn(a_ref[0, PAIR * pair + at], dout_low * halves[at])
        derror_low = derror.astype(BF16)
        dtarget = derror
        for at in range(PAIR):
            dtarget = dtarget + mm_tn(t_ref[0, PAIR * pair + at], derror_low * halves[at])
        dtarget_low = dtarget.astype(BF16)
        dproj_ref[:, spot(2)] = (-dtarget).astype(BF16)
        both = jnp.concatenate([s_ref[0, pair], first[pair]], axis=0)
        from_out = mm_nt(dout_low, both)
        from_target = mm_nt(dtarget_low, both)
        dquery = jnp.where(carried > 0.5, from_out[:, :LANES], from_out[:, LANES:])
        dkey = jnp.where(carried > 0.5, from_target[:, :LANES], from_target[:, LANES:])
        dscaled = -final * mm_nt(error, upper_low)
        for at in range(PAIR):
            dscore = (-causal * mm_nt(dout_low * halves[at], error)).astype(BF16)
            dlower = (-earlier * mm_nt(dtarget_low * halves[at], error)).astype(BF16)
            part = scaled_key * halves[at]
            dquery = dquery + mm(dscore, part)
            dkey = dkey + mm(dlower, part)
            dscaled = dscaled + mm_tn(dscore, query * halves[at]) + mm_tn(dlower, key * halves[at])
        dkey = dkey + rate * dscaled
        dproj_ref[:, spot(0)] = dquery.astype(BF16)
        dproj_ref[:, spot(1)] = dkey.astype(BF16)
        row_head = lax.broadcasted_iota(jnp.int32, (LANES, LANES), 0) // HEAD_DIM
        col = lax.broadcasted_iota(jnp.int32, (LANES, LANES), 1)
        pick = jnp.where(col == PAIR * pair + row_head, 1.0, 0.0).astype(BF16)
        drate = drate + mm_split(dscaled * key_wide, pick)
        rows = jnp.concatenate([key, query], axis=0)
        carried_low = carried.astype(BF16)
        carried_both = jnp.concatenate([carried_low, carried_low], axis=0)
        kept = rows * carried_both
        sides = jnp.concatenate([kept, rows - kept], axis=1)
        pulled = mm_tn(sides, jnp.concatenate([dtarget_low, dout_low], axis=0))
        grad[pair] = keep * upper + block * pulled[:LANES]
        dfirst[pair] += (1.0 - keep) * upper + block * pulled[LANES:]
    dproj_ref[:, 4 * width :] = (
        drate * rates * (1.0 - rates) * (1.0 / (MINIBATCH * HEAD_DIM))
    ).astype(BF16)

    @pl.when(step == chunks - 1)
    def _():
        for pair in range(pairs):
            dinit_ref[PAIR * pair] = dfirst[pair, :HEAD_DIM, :HEAD_DIM]
            dinit_ref[PAIR * pair + 1] = dfirst[pair, HEAD_DIM:, HEAD_DIM:]


MESH = pl.DeviceIdType.MESH


def chip_peer(hops):
    me = lax.axis_index("head")
    chips = lax.axis_size("head") // 2
    return {"head": lax.rem(me // 2 + hops, chips) * 2 + lax.rem(me, 2)}


def core_peer():
    me = lax.axis_index("head")
    return {"head": me + 1 - 2 * lax.rem(me, 2)}


def head_peer(ahead):
    return {"head": lax.rem(lax.axis_index("head") + ahead, lax.axis_size("head"))}


def mlp_peer(flip):
    me = lax.axis_index("mlp")
    across, along = lax.rem(me, 2), me // 2
    if flip % 2:
        across = 1 - across
    if flip // 2:
        along = 1 - along
    return {"mlp": 2 * along + across}


def greet(peers):
    barrier = pltpu.get_barrier_semaphore()
    for peer in peers:
        pl.semaphore_signal(barrier, inc=1, device_id=peer, device_id_type=MESH)
    pl.semaphore_wait(barrier, len(peers))


def copies_of(moves, send_sems, recv_sems, base=0):
    made = []
    for at, (source, target, peer) in enumerate(moves, base):
        if peer is None:
            made.append(pltpu.make_async_copy(source, target, send_sems.at[at]))
        else:
            made.append(
                pltpu.make_async_remote_copy(
                    src_ref=source,
                    dst_ref=target,
                    send_sem=send_sems.at[at],
                    recv_sem=recv_sems.at[at],
                    device_id=peer,
                    device_id_type=MESH,
                )
            )
    return made


def launch(moves, send_sems, recv_sems, base=0):
    for copy in copies_of(moves, send_sems, recv_sems, base):
        copy.start()


def settle(moves, send_sems, recv_sems, base=0):
    for copy in copies_of(moves, send_sems, recv_sems, base):
        copy.wait()


def anywhere(count):
    return [pl.BlockSpec(memory_space=pl.ANY)] * count


def sem_pair(count):
    return [pltpu.SemaphoreType.DMA((count,)), pltpu.SemaphoreType.DMA((count,))]


def gather_parts(moves, sems):
    copies = [
        pltpu.make_async_copy(source, target, sems.at[at])
        for at, (source, target) in enumerate(moves)
    ]
    for copy in copies:
        copy.start()
    for copy in copies:
        copy.wait()


def near_peers():
    return [mlp_peer(flip) for flip in (1, 2, 3)]


def line_peers():
    return [chip_peer(hops) for hops in (1, 2, 3)]


def line_moves(values, begin, target):
    size = values.shape[0] // 2
    part = values.at[pl.ds(begin * size, size)]
    peers = line_peers()
    return [(part, target.at[pl.ds(at * size, size)], peers[at]) for at in range(3)]


class Carry:
    def __init__(self, arrays=(), out_shape=(), plan=None, count=1, collective_id=None, later=None):
        self.arrays = list(arrays)
        self.out_shape = [jax.ShapeDtypeStruct(shape, BF16) for shape in out_shape]
        self.plan = plan
        self.count = count
        self.collective_id = collective_id
        self.later = later

    def params(self):
        extra = {}
        if self.plan is not None:
            extra = {"collective_id": self.collective_id, "has_side_effects": True}
        return pltpu.CompilerParams(vmem_limit_bytes=VMEM_MOST, **extra)

    def split(self, refs, ins, outs):
        mine, given = len(self.arrays), len(self.out_shape)
        body = refs[:ins] + refs[ins + mine : ins + mine + outs] + refs[ins + mine + outs + given : -2]
        extra_in = refs[ins : ins + mine]
        extra_out = refs[ins + mine + outs : ins + mine + outs + given]
        return body, extra_in, extra_out, refs[-2], refs[-1]

    def wrap(self, body, ins, outs):
        def kernel(*refs):
            own, extra_in, extra_out, send_sems, recv_sems = self.split(refs, ins, outs)
            if self.plan is not None:

                @pl.when(pl.program_id(0) == 0)
                def _():
                    peers, moves = self.plan(extra_in, extra_out)
                    greet(peers)
                    launch(moves, send_sems, recv_sems)

            if self.later is not None:

                @pl.when(pl.program_id(0) == self.later[0])
                def _():
                    moves = self.plan(extra_in, extra_out)[1]
                    settle(moves[: self.later[1]], send_sems, recv_sems)
                    launch(self.later[2](extra_in, extra_out), send_sems, recv_sems, len(moves))

            body(*own)
            if self.plan is not None:

                @pl.when(pl.program_id(0) == pl.num_programs(0) - 1)
                def _():
                    moves = self.plan(extra_in, extra_out)[1]
                    done = 0 if self.later is None else self.later[1]
                    settle(moves[done:], send_sems, recv_sems, done)
                    if self.later is not None:
                        settle(self.later[2](extra_in, extra_out), send_sems, recv_sems, len(moves))

        return kernel


def mixer_forward(lengths, proj, initial, gains, biases, carry):
    rows = proj.shape[0]
    heads = initial.shape[0]
    width = heads * HEAD_DIM
    chunks = rows // CHUNK
    pairs = heads // PAIR
    full = lambda *shape: pl.BlockSpec(shape, lambda c: (0,) * len(shape))
    got = pl.pallas_call(
        carry.wrap(forward_kernel, 5, 6),
        grid=(chunks,),
        in_specs=[
            pl.BlockSpec(memory_space=pltpu.SMEM),
            pl.BlockSpec((CHUNK, proj.shape[1]), lambda c: (c, 0)),
            full(heads, HEAD_DIM, HEAD_DIM),
            full(1, width),
            full(1, width),
            *anywhere(len(carry.arrays)),
        ],
        out_specs=[
            pl.BlockSpec((CHUNK, width), lambda c: (c, 0)),
            pl.BlockSpec((CHUNK, width), lambda c: (c, 0)),
            pl.BlockSpec((CHUNK, width), lambda c: (c, 0)),
            pl.BlockSpec((1, pairs, LANES, LANES), lambda c: (c, 0, 0, 0)),
            pl.BlockSpec((1, heads, CHUNK, CHUNK), lambda c: (c, 0, 0, 0)),
            pl.BlockSpec((1, heads, CHUNK, CHUNK), lambda c: (c, 0, 0, 0)),
            *anywhere(len(carry.out_shape)),
        ],
        out_shape=[
            jax.ShapeDtypeStruct((rows, width), BF16),
            jax.ShapeDtypeStruct((rows, width), BF16),
            jax.ShapeDtypeStruct((rows, width), F32),
            jax.ShapeDtypeStruct((chunks, pairs, LANES, LANES), BF16),
            jax.ShapeDtypeStruct((chunks, heads, CHUNK, CHUNK), BF16),
            jax.ShapeDtypeStruct((chunks, heads, CHUNK, CHUNK), BF16),
            *carry.out_shape,
        ],
        scratch_shapes=[
            pltpu.VMEM((pairs, LANES, LANES), F32),
            pltpu.VMEM((pairs, LANES, LANES), F32),
            *sem_pair(carry.count),
        ],
        compiler_params=carry.params(),
        cost_estimate=pl.CostEstimate(
            flops=rows * width * CHUNK * 40, bytes_accessed=rows * width * 30, transcendentals=rows * width
        ),
        name="mixer_forward",
    )(lengths, proj, initial, gains, biases, *carry.arrays)
    return got[:6], got[6:]


def mixer_backward(lengths, dmixed, proj, initial, gains, biases, kept, carry, places=(0, 0)):
    rows = proj.shape[0]
    heads = initial.shape[0]
    width = heads * HEAD_DIM
    chunks = rows // CHUNK
    pairs = heads // PAIR
    full = lambda *shape: pl.BlockSpec(shape, lambda i: (0,) * len(shape))
    at = lambda *shape: pl.BlockSpec(shape, lambda i: (chunks - 1 - i,) + (0,) * (len(shape) - 1))
    got = pl.pallas_call(
        carry.wrap(backward_kernel, 11, 4),
        grid=(chunks,),
        in_specs=[
            pl.BlockSpec(memory_space=pltpu.SMEM),
            at(CHUNK, width),
            at(CHUNK, proj.shape[1]),
            full(heads, HEAD_DIM, HEAD_DIM),
            pl.BlockSpec((1, width), lambda i: (0, places[0])),
            pl.BlockSpec((1, width), lambda i: (0, places[1])),
            at(CHUNK, width),
            at(CHUNK, width),
            at(1, pairs, LANES, LANES),
            at(1, heads, CHUNK, CHUNK),
            at(1, heads, CHUNK, CHUNK),
            *anywhere(len(carry.arrays)),
        ],
        out_specs=[
            at(CHUNK, proj.shape[1]),
            full(heads, HEAD_DIM, HEAD_DIM),
            full(1, width),
            full(1, width),
            *anywhere(len(carry.out_shape)),
        ],
        out_shape=[
            jax.ShapeDtypeStruct(proj.shape, BF16),
            jax.ShapeDtypeStruct((heads, HEAD_DIM, HEAD_DIM), F32),
            jax.ShapeDtypeStruct((1, width), F32),
            jax.ShapeDtypeStruct((1, width), F32),
            *carry.out_shape,
        ],
        scratch_shapes=[
            pltpu.VMEM((pairs, LANES, LANES), F32),
            pltpu.VMEM((pairs, LANES, LANES), BF16),
            pltpu.VMEM((pairs, LANES, LANES), F32),
            *sem_pair(carry.count),
        ],
        compiler_params=carry.params(),
        cost_estimate=pl.CostEstimate(
            flops=rows * width * CHUNK * 50, bytes_accessed=rows * width * 40, transcendentals=rows * width
        ),
        name="mixer_backward",
    )(lengths, dmixed, proj, initial, gains, biases, *kept, *carry.arrays)
    return got[:4], got[4:]


def head_kernel(*refs):
    len_ref, tokens, rate_rows, init_ref = refs[:4]
    vectors, (weight_raw, cot, out_weight), refs = refs[4:8], refs[8:11], refs[11:]
    proj_ref, rate, mixed_ref, e_ref, z_ref, s_ref, t_ref, a_ref, gain = refs[:9]
    gathered_ref, cot_got, weight_ref, mixed_rows, out_cross, out_other, cot_line, out_line = refs[9:17]
    held, raw, weight, state, first, slots, line_hold, own_hold = refs[17:25]
    line_send, line_recv, core_send, core_recv, near_send, near_recv, out_send, out_recv = refs[25:33]
    keep_sem, weight_sem, row_send, row_recv, cross_send, cross_recv = refs[33:39]
    cot_send, cot_recv, other_send, other_recv, hold_sems = refs[39:]
    me = lax.axis_index("head")
    chip, core = me // 2, lax.rem(me, 2)
    member = lax.axis_index("mlp")
    rows = tokens.shape[0]
    chips = held.shape[0] // (2 * rows)
    sides = [mlp_peer(flip) for flip in (1, 2, 3)]
    others = [chip_peer(hops) for hops in range(1, chips)]
    partner = core_peer()
    load = pltpu.make_async_copy(weight_raw, raw, weight_sem.at[0])
    load.start()
    place_at = 0
    for vector in vectors:
        values = vector[...].astype(F32)
        for at in range(vector.shape[0]):
            gain[:, place_at : place_at + LANES] = values[at : at + 1, :]
            place_at += LANES
    source = tokens[...].astype(F32)
    own_rows = pl.ds(pl.multiple_of(me * rows, rows), rows)
    held[own_rows, :] = (source * rms_scale(source) * gain[:, : source.shape[1]]).astype(BF16)
    rate[...] = jnp.zeros_like(rate)
    rate[: rate_rows.shape[0], :] = rate_rows[...]
    greet([head_peer(ahead) for ahead in range(1, 8)] + sides)

    def place(of_chip, of_core):
        return held.at[pl.ds(pl.multiple_of((of_chip * 2 + of_core) * rows, rows), rows)]

    def hop(of_chip, step):
        side = (step + 1) // 2
        return pltpu.make_async_remote_copy(
            src_ref=place(of_chip, core),
            dst_ref=place(of_chip, core),
            send_sem=line_send.at[side, of_chip],
            recv_sem=line_recv.at[of_chip],
            device_id={"head": me + 2 * step},
            device_id_type=MESH,
        )

    def across(of_chip, of_core):
        return pltpu.make_async_remote_copy(
            src_ref=place(of_chip, of_core),
            dst_ref=place(of_chip, of_core),
            send_sem=core_send.at[of_chip],
            recv_sem=core_recv.at[of_chip],
            device_id=partner,
            device_id_type=MESH,
        )

    quarter = out_weight.shape[0] // 4
    part = out_weight.at[pl.ds(pl.multiple_of(member * quarter, quarter), quarter)]
    near_moves = [(cot, cot_got.at[at], sides[at]) for at in range(3)]
    out_moves = [(part, out_line.at[chip], peer) for peer in others]
    for step in (-1, 1):

        @pl.when(jnp.logical_and(chip + step >= 0, chip + step < chips))
        def _(step=step):
            hop(chip, step).start()

    across(chip, core).start()
    launch(near_moves, near_send, near_recv)
    def product(of_chip):
        block = pl.ds(pl.multiple_of(of_chip * 2 * rows, 2 * rows), 2 * rows)
        values = held[block, :]
        wide = weight.shape[1]
        proj_ref[block, :wide] = jnp.dot(values, weight[...], preferred_element_type=F32)
        proj_ref[block, wide:] = mm_nt(values, rate[...])
        pltpu.make_async_copy(held.at[block], gathered_ref.at[block], keep_sem.at[of_chip]).start()

    def turn(at):
        if isinstance(at, int) and at == 0:
            return chip
        if isinstance(at, int) and at == 1:
            return chip + 1 - 2 * lax.rem(chip, 2)
        return at - (2 * at - 3) * (chip // 2)

    def arrive(at):
        of_chip = turn(at)
        pltpu.make_async_remote_copy(
            src_ref=place(of_chip, core),
            dst_ref=place(of_chip, core),
            send_sem=line_send.at[0, of_chip],
            recv_sem=line_recv.at[of_chip],
            device_id=partner,
            device_id_type=MESH,
        ).wait_recv()
        for step in (-1, 1):
            wanted = (of_chip > chip) if step < 0 else (of_chip < chip)

            @pl.when(jnp.logical_and(wanted, jnp.logical_and(chip + step >= 0, chip + step < chips)))
            def _(step=step):
                hop(of_chip, step).start()

        across(of_chip, core).start()

    near = sides
    heads = 2 * chips
    ahead = [lax.rem(chip + hops, 4) for hops in (1, 2, 3)]
    local = mixed_ref.shape[1]
    half = quarter // 2
    top, bottom = pl.ds(0, half), pl.ds(half, half)

    def row_copy(sender, target, stays):
        rel = lax.rem(core + target, 2)
        place_at = mixed_rows.at[rel, :, pl.ds(pl.multiple_of(chip * local, local), local)]
        if stays:
            return pltpu.make_async_copy(slots.at[target], place_at, row_send.at[target])
        return pltpu.make_async_remote_copy(
            src_ref=slots.at[target],
            dst_ref=place_at,
            send_sem=row_send.at[target],
            recv_sem=row_recv.at[sender],
            device_id={"head": target},
            device_id_type=MESH,
        )

    def cross_moves(flip):
        if flip < 2:
            return [
                (out_line.at[of_chip], out_cross.at[of_chip, member], near[flip])
                for of_chip in ahead
            ]
        moves = []
        for of_chip in ahead:
            one = out_cross.at[of_chip, near[0]["mlp"], top]
            two = out_cross.at[of_chip, near[1]["mlp"], bottom]
            moves += [(one, one, near[1]), (two, two, near[0])]
        return moves

    def swap_moves(flip):
        of_member = near[flip]["mlp"]
        return [
            (out_cross.at[of_chip, of_member], out_other.at[of_chip, of_member], partner)
            for of_chip in ahead
        ]

    def hold_moves():
        moves = [(line_hold.at[at], out_cross.at[ahead[at], member], None) for at in range(3)]
        moves += [(line_hold.at[at], out_other.at[ahead[at], member], partner) for at in range(3)]
        return moves + [
            (own_hold, out_cross.at[chip], None),
            (own_hold, out_other.at[chip], partner),
        ]

    cot_moves = line_moves(cot, 0, cot_line)
    own_out = [
        pltpu.make_async_copy(
            out_weight.at[pl.ds(at * quarter, quarter)], own_hold.at[at], hold_sems.at[3 + at]
        )
        for at in range(4)
    ]
    for copy in own_out:
        copy.start()

    def local_part(of_chip):
        for of_core in range(2):
            at = of_chip * 2 + of_core
            block = pl.ds(pl.multiple_of(at * CHUNK, CHUNK), CHUNK)
            one = pl.ds(at, 1)
            forward_local(len_ref, proj_ref.at[block], t_ref.at[one], a_ref.at[one], at)

    inner = jnp.logical_and(chip > 0, chip < chips - 1)
    outer = jnp.logical_not(inner)
    arrive(1)
    pl.when(inner)(lambda: arrive(2))
    launch(out_moves, out_send, out_recv)
    load.wait()
    wide = raw.shape[2]

    def untie(at, _):
        span = pl.ds(pl.multiple_of(at * 256, 256), 256)
        values = raw[span]
        for part in range(4):
            weight[span, part * wide : (part + 1) * wide] = values[:, part, :]
        return 0

    lax.fori_loop(0, raw.shape[0] // 256, untie, 0)
    store = pltpu.make_async_copy(weight, weight_ref, weight_sem.at[1])
    store.start()

    def gather_step(at, _):
        pl.when(jnp.logical_and(inner, at == 1))(lambda: arrive(3))
        pl.when(jnp.logical_and(outer, at == 2))(lambda: arrive(2))
        pl.when(jnp.logical_and(outer, at == 3))(lambda: arrive(3))

        @pl.when(at == 2)
        def _():
            settle(out_moves, out_send, out_recv)
            for flip in range(2):
                launch(cross_moves(flip), cross_send.at[flip], cross_recv.at[flip])
            gather_parts(
                [(out_line.at[ahead[spot]], line_hold.at[spot]) for spot in range(3)], hold_sems
            )
            for copy in own_out:
                copy.wait()
            launch(hold_moves(), other_send.at[3], other_recv.at[3])

        @pl.when(at == 3)
        def _():
            launch(cot_moves, cot_send, cot_recv)

        of_chip = jnp.where(at == 0, turn(0), jnp.where(at == 1, turn(1), turn(at)))
        across(of_chip, 1 - core).wait_recv()
        product(of_chip)
        local_part(of_chip)
        return 0

    lax.fori_loop(0, chips, gather_step, 0)

    def rows_of(at):
        return pl.ds(pl.multiple_of(at * CHUNK, CHUNK), CHUNK)

    def advance(at):
        block, one = rows_of(at), pl.ds(at, 1)
        return forward_state(
            len_ref,
            proj_ref.at[block],
            init_ref,
            e_ref.at[block],
            z_ref.at[block],
            s_ref.at[one],
            t_ref.at[one],
            a_ref.at[one],
            state,
            first,
            at,
        )

    spot = 2 * tokens.shape[1]
    mix_gain = gain.at[:, pl.ds(spot, local)]
    mix_bias = gain.at[:, pl.ds(spot + local, local)]

    def ship(at):
        mixed_ref[rows_of(at), :] = slots[at]

        @pl.when(at != me)
        def _():
            row_copy(me, at, False).start()

        @pl.when(at == me)
        def _():
            row_copy(me, at, True).start()

    def step(at, outs):
        @pl.when(at == 1)
        def _():
            for flip in range(2):
                settle(cross_moves(flip), cross_send.at[flip], cross_recv.at[flip])
            launch(cross_moves(2), cross_send.at[2], cross_recv.at[2])
            for flip in range(2):
                launch(swap_moves(flip), other_send.at[flip], other_recv.at[flip])

        gates = proj_ref[rows_of(at - 1), 3 * local : 4 * local]
        later = advance(at)
        forward_tail(outs, gates, mix_gain, mix_bias, slots.at[at - 1])
        ship(at - 1)
        return tuple(later)

    outs = lax.fori_loop(1, heads, step, tuple(advance(0)))
    gates = proj_ref[rows_of(heads - 1), 3 * local : 4 * local]
    forward_tail(outs, gates, mix_gain, mix_bias, slots.at[heads - 1])
    ship(heads - 1)
    settle(cross_moves(2), cross_send.at[2], cross_recv.at[2])
    launch(swap_moves(2), other_send.at[2], other_recv.at[2])
    settle(cot_moves, cot_send, cot_recv)
    settle(hold_moves(), other_send.at[3], other_recv.at[3])
    for at in range(8):

        @pl.when(me != at)
        def _(at=at):
            row_copy(me, at, False).wait_send()
            row_copy(at, at, False).wait_recv()

        @pl.when(me == at)
        def _(at=at):
            row_copy(me, at, True).wait()

    for at in range(chips):
        of_chip = turn(at)
        across(of_chip, core).wait_send()
        block = pl.ds(pl.multiple_of(of_chip * 2 * rows, 2 * rows), 2 * rows)
        pltpu.make_async_copy(held.at[block], gathered_ref.at[block], keep_sem.at[of_chip]).wait()
        for step in (-1, 1):
            wanted = (of_chip >= chip) if step < 0 else (of_chip <= chip)

            @pl.when(jnp.logical_and(wanted, jnp.logical_and(chip + step >= 0, chip + step < chips)))
            def _(step=step):
                hop(of_chip, step).wait_send()

    settle(near_moves, near_send, near_recv)
    store.wait()
    for flip in range(3):
        settle(swap_moves(flip), other_send.at[flip], other_recv.at[flip])


def head(lengths, tokens, rate_rows, initial, vectors, in_weight, cot, out_weight, collective_id):
    devices = lax.axis_size("head")
    rows, width = tokens.shape
    heads = initial.shape[0]
    local = heads * HEAD_DIM
    pairs = heads // PAIR
    wide = 4 * in_weight.shape[2]
    chips = devices // 2
    quarters = (4, out_weight.shape[0] // 4, width)
    vmem = pl.BlockSpec(memory_space=pltpu.VMEM)
    got = pl.pallas_call(
        head_kernel,
        in_specs=[pl.BlockSpec(memory_space=pltpu.SMEM)] + [vmem] * 7 + anywhere(3),
        out_specs=[vmem] * 9 + anywhere(8),
        out_shape=[
            jax.ShapeDtypeStruct((devices * rows, wide + LANES), F32),
            jax.ShapeDtypeStruct((LANES, width), BF16),
            jax.ShapeDtypeStruct((devices * rows, local), BF16),
            jax.ShapeDtypeStruct((devices * rows, local), BF16),
            jax.ShapeDtypeStruct((devices * rows, local), F32),
            jax.ShapeDtypeStruct((devices, pairs, LANES, LANES), BF16),
            jax.ShapeDtypeStruct((devices, heads, CHUNK, CHUNK), BF16),
            jax.ShapeDtypeStruct((devices, heads, CHUNK, CHUNK), BF16),
            jax.ShapeDtypeStruct((1, sum(vector.size for vector in vectors)), F32),
            jax.ShapeDtypeStruct((devices * rows, width), BF16),
            jax.ShapeDtypeStruct((3, rows, width), BF16),
            jax.ShapeDtypeStruct((width, wide), BF16),
            jax.ShapeDtypeStruct((2, rows, width // 2), BF16),
            jax.ShapeDtypeStruct((4, *quarters), BF16),
            jax.ShapeDtypeStruct((4, *quarters), BF16),
            jax.ShapeDtypeStruct((3 * rows // 2, width), BF16),
            jax.ShapeDtypeStruct((chips, *quarters[1:]), BF16),
        ],
        scratch_shapes=[
            pltpu.VMEM((devices * rows, width), BF16),
            pltpu.VMEM(in_weight.shape, BF16),
            pltpu.VMEM((width, wide), BF16),
            pltpu.VMEM((pairs, LANES, LANES), F32),
            pltpu.VMEM((pairs, LANES, LANES), F32),
            pltpu.VMEM((devices, CHUNK, local), BF16),
            pltpu.VMEM((3, *quarters[1:]), BF16),
            pltpu.VMEM(quarters, BF16),
            pltpu.SemaphoreType.DMA((2, chips)),
            pltpu.SemaphoreType.DMA((chips,)),
            pltpu.SemaphoreType.DMA((chips,)),
            pltpu.SemaphoreType.DMA((chips,)),
            *sem_pair(3),
            *sem_pair(3),
            pltpu.SemaphoreType.DMA((chips,)),
            pltpu.SemaphoreType.DMA((2,)),
            *sem_pair(8),
            pltpu.SemaphoreType.DMA((3, 6)),
            pltpu.SemaphoreType.DMA((3, 6)),
            *sem_pair(3),
            pltpu.SemaphoreType.DMA((4, 8)),
            pltpu.SemaphoreType.DMA((4, 8)),
            pltpu.SemaphoreType.DMA((7,)),
        ],
        compiler_params=pltpu.CompilerParams(
            vmem_limit_bytes=VMEM_MOST, collective_id=collective_id, has_side_effects=True
        ),
        cost_estimate=pl.CostEstimate(
            flops=2 * devices * rows * width * wide, bytes_accessed=4 * devices * rows * width, transcendentals=0
        ),
        name="head",
    )(lengths, tokens, rate_rows, initial, *vectors, in_weight, cot, out_weight)
    return got[:2], got[2:8], got[8], got[9:16]


UNITS = 704
PLANE_UNITS = 688
SPAN = 512
FINISH = 176


def gated(gate, up):
    sigmoid = jax.nn.sigmoid(gate)
    silu = gate * sigmoid
    return silu, sigmoid + silu * (1.0 - sigmoid)


def tile(*shape):
    return pl.BlockSpec(shape, (lambda i: (0, i, 0)) if len(shape) == 3 else (lambda i: (i, 0)))


def plane_kernel(*refs):
    x_own, x_got, o_own, o_got, gu_ref, down_ref, dx_ref, out_ref = refs[:8]
    act_ref, d_gate_ref, d_up_ref, x_all, o_all, dx_sum, out_sum, turned, sems = refs[8:]
    rows = x_own.shape[0]
    step = pl.program_id(0)
    last = pl.num_programs(0) - 1

    @pl.when(step == 0)
    def _():
        moves = [(x_own, x_all.at[pl.ds(0, rows)]), (o_own, o_all.at[pl.ds(0, rows)])]
        for at in range(3):
            place = pl.ds((at + 1) * rows, rows)
            moves += [(x_got.at[at], x_all.at[place]), (o_got.at[at], o_all.at[place])]
        gather_parts(moves, sems)

    gate = mm_nt(gu_ref[0], x_all[...])
    up = mm_nt(gu_ref[1], x_all[...])
    d_act = mm_nt(down_ref[...], o_all[...])
    silu, slope = gated(gate, up)
    act = (silu * up).astype(BF16)
    d_gate = (d_act * up * slope).astype(BF16)
    d_up = (d_act * silu).astype(BF16)
    act_ref[...] = act
    d_gate_ref[...] = d_gate
    d_up_ref[...] = d_up
    for at, part in enumerate((d_gate, d_up, act)):
        turned[at] = part.T

    def back(at, _):
        span = pl.ds(pl.multiple_of(at * SPAN, SPAN), SPAN)
        dx = mm(turned[0], gu_ref[0, :, span]) + mm(turned[1], gu_ref[1, :, span])
        out = mm(turned[2], down_ref[:, span])

        @pl.when(step == 0)
        def _():
            dx_sum[:, span] = dx
            out_sum[:, span] = out

        @pl.when(step > 0)
        def _():
            dx_sum[:, span] += dx
            out_sum[:, span] += out

        @pl.when(step == last)
        def _():
            for at in range(4):
                place = pl.ds(at * rows, rows)
                dx_ref[at, :, span] = dx_sum[place, span].astype(BF16)
                out_ref[at, :, span] = out_sum[place, span].astype(BF16)

        return 0

    lax.fori_loop(0, x_all.shape[1] // SPAN, back, 0)


def mlp_plane(x_own, x_got, o_own, o_got, gate_up_rows, down_weight, carry):
    rows, width = x_own.shape
    hidden = down_weight.shape[0]
    whole = pl.BlockSpec((4, rows, width), lambda i: (0, 0, 0))
    got = pl.pallas_call(
        carry.wrap(plane_kernel, 6, 5),
        grid=(hidden // PLANE_UNITS,),
        in_specs=anywhere(4)
        + [tile(2, PLANE_UNITS, width), tile(PLANE_UNITS, width)]
        + anywhere(len(carry.arrays)),
        out_specs=[whole, whole]
        + [tile(PLANE_UNITS, 4 * rows)] * 3
        + anywhere(len(carry.out_shape)),
        out_shape=[jax.ShapeDtypeStruct((4, rows, width), BF16)] * 2
        + [jax.ShapeDtypeStruct((hidden, 4 * rows), BF16)] * 3
        + carry.out_shape,
        scratch_shapes=[
            pltpu.VMEM((4 * rows, width), BF16),
            pltpu.VMEM((4 * rows, width), BF16),
            pltpu.VMEM((4 * rows, width), F32),
            pltpu.VMEM((4 * rows, width), F32),
            pltpu.VMEM((3, 4 * rows, PLANE_UNITS), BF16),
            pltpu.SemaphoreType.DMA((8,)),
            *sem_pair(carry.count),
        ],
        compiler_params=carry.params(),
        cost_estimate=pl.CostEstimate(
            flops=48 * rows * hidden * width, bytes_accessed=6 * hidden * width, transcendentals=4 * rows * hidden
        ),
        name="mlp_plane",
    )(x_own, x_got, o_own, o_got, gate_up_rows, down_weight, *carry.arrays)
    return got[:2], got[2:5], got[5:]


def grads_kernel(*refs):
    x_own, x_got, x_far, o_own, o_got, o_far = refs[0], refs[1], refs[2:10], refs[10], refs[11], refs[12:20]
    in_part, out_part, back_part, gu_hbm, down_hbm = refs[20:25]
    plane_acts, small_ref, init_ref = refs[25:28], refs[28], refs[29]
    own_gu, own_down, far_gu, far_down, in_all, out_all = refs[30:36]
    core_got, back_got, back_own, small_out, gains_out, init_out = refs[36:42]
    x_all, o_all, act, d_gate, d_up, gu_ref, down_ref, slots = refs[42:50]
    back_low, back_load, small_got, gains_got, init_got = refs[50:55]
    in_bufs, out_bufs = refs[55:61], refs[61:67]
    load_sems, sum_sems, tile_send, tile_recv, phase_send, phase_recv = refs[67:]
    step = pl.program_id(0)
    rows, width = x_all.shape
    me = lax.axis_index("head")
    chip, core = me // 2, lax.rem(me, 2)
    member = lax.axis_index("mlp")
    partner = core_peer()
    near = near_peers()
    across, along = near[0], near[1]
    others = [head_peer(ahead) for ahead in range(1, 8)]
    hidden = own_gu.shape[1]
    sides = ((in_part, in_all, in_bufs), (out_part, out_all, out_bufs))

    def piece(part, of_member, half):
        size = part.shape[0] // 8
        return part.at[pl.ds(pl.multiple_of(of_member * 2 * size + half * size, size), size)]

    def quick_moves():
        moves = [(back_part.at[:, 1 - core], core_got, partner)]
        for at in range(3):
            moves.append((small_ref, small_got.at[at], near[at]))
            moves.append((init_ref, init_got.at[at], near[at]))
        return moves

    def line_sums():
        moves = [(back_low.at[chip], back_own, None)]
        for hops in range(1, 4):
            moves.append(
                (back_low.at[lax.rem(chip + hops, 4)], back_got.at[hops - 1], chip_peer(hops))
            )
        gains = small_out.at[pl.ds(0, 8)]
        return moves + [(gains, gains_got.at[at], others[at]) for at in range(7)]

    def reduce_one():
        moves = []
        for part, _, (got, _, _, _, _, _) in sides:
            moves.append((piece(part, near[0]["mlp"], 0), got.at[0], across))
            moves.append((piece(part, near[2]["mlp"], 0), got.at[1], across))
            moves.append((piece(part, near[1]["mlp"], 1), got.at[2], along))
            moves.append((piece(part, near[2]["mlp"], 1), got.at[3], along))
        return moves

    def reduce_two():
        moves = []
        for _, _, (_, _, passed, _, got, _) in sides:
            moves += [(passed.at[0], got.at[0], along), (passed.at[1], got.at[1], across)]
        return moves

    def spread_one():
        moves = []
        for _, whole, (_, _, _, _, _, total) in sides:
            moves += [(total, whole.at[member], peer) for peer in (across, along, None)]
        return moves

    def spread_two():
        moves = []
        for _, whole, _ in sides:
            half = whole.shape[1] // 2
            top = whole.at[across["mlp"], pl.ds(0, half)]
            bottom = whole.at[along["mlp"], pl.ds(half, half)]
            moves += [(top, top, along), (bottom, bottom, across)]
        return moves

    phases = [quick_moves, line_sums, reduce_one, reduce_two, spread_one, spread_two]

    def begin(at):
        launch(phases[at](), phase_send.at[at], phase_recv.at[at])

    def end(at):
        settle(phases[at](), phase_send.at[at], phase_recv.at[at])

    near_rows = x_own.shape[0]
    plane_rows = 4 * near_rows
    piece_rows = (rows - plane_rows) // 8
    sizes = (UNITS, hidden - UNITS)

    def weight_moves(at):
        span, size = pl.ds(at * UNITS, sizes[at]), pl.ds(0, sizes[at])
        return [(gu_hbm.at[:, span], gu_ref.at[:, size]), (down_hbm.at[span], down_ref.at[size])]

    def act_moves(at):
        span, size = pl.ds(at * UNITS, sizes[at]), pl.ds(0, sizes[at])
        return [
            (part.at[span], whole.at[size, pl.ds(0, plane_rows)])
            for part, whole in zip(plane_acts, (act, d_gate, d_up))
        ]

    def far_moves(begin, end):
        moves = []
        for at in range(begin, end):
            place = pl.ds(plane_rows + at * piece_rows, piece_rows)
            moves += [(x_far[at], x_all.at[place]), (o_far[at], o_all.at[place])]
        return moves

    def near_moves():
        moves = []
        for own, got, whole in ((x_own, x_got, x_all), (o_own, o_got, o_all)):
            moves.append((own, whole.at[pl.ds(0, near_rows)]))
            for at in range(3):
                moves.append((got.at[at], whole.at[pl.ds((at + 1) * near_rows, near_rows)]))
        return moves

    groups = [far_moves(0, 3), far_moves(3, 6), far_moves(6, 8), near_moves()]
    bases = [5, 11, 17, 21]

    def loads(moves, base):
        return [
            pltpu.make_async_copy(source, target, load_sems.at[base + at])
            for at, (source, target) in enumerate(moves)
        ]

    def fetch(moves, base):
        for copy in loads(moves, base):
            copy.start()

    def fetched(moves, base):
        for copy in loads(moves, base):
            copy.wait()

    def chunk_moves(at, column):
        span, size = pl.ds(at * UNITS, sizes[at]), pl.ds(0, sizes[at])
        columns = pl.ds(pl.multiple_of(column * SPAN, SPAN), SPAN)
        slot = slots.at[lax.rem(column, 2)]
        moves = []
        for gu, down, peer in ((own_gu, own_down, None), (far_gu, far_down, partner)):
            moves += [
                (slot.at[0, size], gu.at[0, span, columns], peer),
                (slot.at[1, size], gu.at[1, span, columns], peer),
                (slot.at[2, size], down.at[span, columns], peer),
            ]
        return moves

    def chunk_sems(at, column):
        place = 4 * at + column
        return tile_send.at[place], tile_recv.at[place]

    @pl.when(step == 0)
    def _():
        fetch(weight_moves(0), 0)
        fetch(groups[0], bases[0])
        greet(near + others)
        begin(0)
        begin(2)
        for at in range(1, 4):
            fetch(groups[at], bases[at])
        fetch(act_moves(0), 2)
        fetched(weight_moves(0), 0)

    @pl.when(step == 1)
    def _():
        fetch(act_moves(1), 2)
        fetched(weight_moves(1), 0)

    def reduce_sums():
        parts = []
        for part, _, (_, own, _, _, _, _) in sides:
            parts.append((piece(part, member, 0), own.at[0]))
            parts.append((piece(part, near[1]["mlp"], 0), own.at[1]))
            parts.append((piece(part, member, 1), own.at[2]))
            parts.append((piece(part, near[0]["mlp"], 1), own.at[3]))
        gather_parts(parts, sum_sems)
        end(2)
        for _, _, (got, own, passed, kept, _, _) in sides:
            for half in range(2):
                kept[half] = own[2 * half].astype(F32) + got[2 * half].astype(F32)
                passed[half] = (
                    own[2 * half + 1].astype(F32) + got[2 * half + 1].astype(F32)
                ).astype(BF16)
        begin(3)

    def reduce_totals():
        end(3)
        for _, _, (_, _, _, kept, got, total) in sides:
            size = total.shape[0] // 2
            for half in range(2):
                total[pl.ds(half * size, size), :] = (kept[half] + got[half].astype(F32)).astype(BF16)
        begin(4)

    def spread_rest():
        end(4)
        begin(5)

    def line_totals():
        end(0)

        def add(at, _):
            gather_parts(
                [(core_got.at[at], back_load.at[0]), (back_part.at[at, core], back_load.at[1])],
                sum_sems,
            )
            back_low[at] = (back_load[0].astype(F32) + back_load[1].astype(F32)).astype(BF16)
            return 0

        lax.fori_loop(0, 4, add, 0)
        total, first = small_ref[...], init_ref[...]
        for at in range(3):
            total = total + small_got[at]
            first = first + init_got[at]
        small_out[...] = total
        init_out[...] = first
        begin(1)

    def ahead(at, _):
        for group in range(3):

            @pl.when(jnp.logical_and(step == 0, at == group))
            def _(group=group):
                fetched(groups[group], bases[group])

        pl.when(jnp.logical_and(step == 0, at == 1))(line_totals)
        pl.when(jnp.logical_and(step == 1, at == 1))(reduce_totals)
        span = pl.ds(pl.multiple_of(plane_rows + at * SPAN, SPAN), SPAN)
        rows_in = x_all[span, :]
        gate = mm_nt(gu_ref[0], rows_in)
        up = mm_nt(gu_ref[1], rows_in)
        d_act = mm_nt(down_ref[...], o_all[span, :])
        silu, slope = gated(gate, up)
        act[:, span] = (silu * up).astype(BF16)
        d_gate[:, span] = (d_act * up * slope).astype(BF16)
        d_up[:, span] = (d_act * silu).astype(BF16)
        return 0

    lax.fori_loop(0, (rows - plane_rows) // SPAN, ahead, 0)

    @pl.when(step == 0)
    def _():
        fetch(weight_moves(1), 0)
        fetched(groups[3], bases[3])
        fetched(act_moves(0), 2)

    @pl.when(step == 1)
    def _():
        fetched(act_moves(1), 2)

    def back(at, _):
        pl.when(jnp.logical_and(step == 0, at == 2))(reduce_sums)
        pl.when(jnp.logical_and(step == 1, at == 3))(spread_rest)

        for of_tile in range(2):

            @pl.when(jnp.logical_and(step == of_tile, at >= 2))
            def _(of_tile=of_tile):
                settle(chunk_moves(of_tile, at - 2), *chunk_sems(of_tile, at - 2))

        @pl.when(jnp.logical_and(step == 1, at < 2))
        def _():
            settle(chunk_moves(0, at + 2), *chunk_sems(0, at + 2))

        span = pl.ds(pl.multiple_of(at * SPAN, SPAN), SPAN)
        columns = x_all[:, span]
        slot = lax.rem(at, 2)
        slots[slot, 0] = mm(d_gate[...], columns).astype(BF16)
        slots[slot, 1] = mm(d_up[...], columns).astype(BF16)
        slots[slot, 2] = mm(act[...], o_all[:, span]).astype(BF16)

        for of_tile in range(2):

            @pl.when(step == of_tile)
            def _(of_tile=of_tile):
                launch(chunk_moves(of_tile, at), *chunk_sems(of_tile, at))

        return 0

    lax.fori_loop(0, width // SPAN, back, 0)

    @pl.when(step == 1)
    def _():
        end(1)
        gains = small_out[0:8, :]
        for at in range(7):
            gains = gains + gains_got[at]
        gains_out[...] = gains
        for at in (2, 3):
            settle(chunk_moves(1, at), *chunk_sems(1, at))
        end(5)


def reduce_buffers(part):
    size, width = part.shape[0] // 8, part.shape[1]
    return [
        pltpu.VMEM((4, size, width), BF16),
        pltpu.VMEM((4, size, width), BF16),
        pltpu.VMEM((2, size, width), BF16),
        pltpu.VMEM((2, size, width), F32),
        pltpu.VMEM((2, size, width), BF16),
        pltpu.VMEM((2 * size, width), BF16),
    ]


def mlp_grads(
    x, o, in_part, out_part, back_part, gate_up_rows, down_weight, plane_acts, small, init, collective_id
):
    arrays = [x[0], x[1], *x[2], o[0], o[1], *o[2], in_part, out_part, back_part]
    arrays += [gate_up_rows, down_weight, *plane_acts]
    hidden, width = down_weight.shape
    near = x[0].shape[0]
    rows = 16 * near
    vmem = pl.BlockSpec(memory_space=pltpu.VMEM)
    low = [
        (2, hidden, width),
        (hidden, width),
        (2, hidden, width),
        (hidden, width),
        (4, in_part.shape[0] // 4, in_part.shape[1]),
        (4, out_part.shape[0] // 4, width),
        (4, near, width),
        (3, near, width),
        (near, width),
    ]
    got = pl.pallas_call(
        grads_kernel,
        grid=(2,),
        in_specs=anywhere(len(arrays)) + [vmem, vmem],
        out_specs=anywhere(len(low)) + [vmem, vmem, vmem],
        out_shape=[jax.ShapeDtypeStruct(shape, BF16) for shape in low]
        + [
            jax.ShapeDtypeStruct(small.shape, F32),
            jax.ShapeDtypeStruct((8, width), F32),
            jax.ShapeDtypeStruct(init.shape, F32),
        ],
        scratch_shapes=[
            pltpu.VMEM((rows, width), BF16),
            pltpu.VMEM((rows, width), BF16),
            pltpu.VMEM((UNITS, rows), BF16),
            pltpu.VMEM((UNITS, rows), BF16),
            pltpu.VMEM((UNITS, rows), BF16),
            pltpu.VMEM((2, UNITS, width), BF16),
            pltpu.VMEM((UNITS, width), BF16),
            pltpu.VMEM((2, 3, UNITS, SPAN), BF16),
            pltpu.VMEM((4, near, width), BF16),
            pltpu.VMEM((2, near, width), BF16),
            pltpu.VMEM((3, *small.shape), F32),
            pltpu.VMEM((7, 8, width), F32),
            pltpu.VMEM((3, *init.shape), F32),
            *reduce_buffers(in_part),
            *reduce_buffers(out_part),
            pltpu.SemaphoreType.DMA((29,)),
            pltpu.SemaphoreType.DMA((8,)),
            pltpu.SemaphoreType.DMA((8, 6)),
            pltpu.SemaphoreType.DMA((8, 6)),
            pltpu.SemaphoreType.DMA((6, 11)),
            pltpu.SemaphoreType.DMA((6, 11)),
        ],
        compiler_params=pltpu.CompilerParams(
            vmem_limit_bytes=VMEM_MOST, collective_id=collective_id, has_side_effects=True
        ),
        cost_estimate=pl.CostEstimate(
            flops=11 * rows * hidden * width, bytes_accessed=14 * hidden * width, transcendentals=rows * hidden
        ),
        name="mlp_grads",
    )(*arrays, small, init)
    return got[:6], got[7], got[8], got[9], got[10], got[11]


def dots_kernel(*refs):
    dproj, columns, weight, rate, first_gain, mlp_part, dgain, dbias = refs[:8]
    side_a, side_b, in_part, back_part, small, corner_a, corner_b, send, recv = refs[8:]
    step = pl.program_id(0)
    wide = weight.shape[1]
    near = near_peers()[:2]
    moves = [(side_a, corner_a, near[1]), (side_b, corner_b, near[0])]

    @pl.when(step == 0)
    def _():
        greet(near)
        launch(moves, send, recv)

    in_part[...] = mm_tn(columns[...], dproj[:, :wide]).astype(BF16)
    rates = mm_tn(dproj[:, wide:], columns[...])
    back = mm_nt(dproj[:, :wide], weight[...]) + mm(dproj[:, wide:], rate[...])
    back_part[...] = back.astype(BF16)
    gains = jnp.sum(back * columns[...].astype(F32), axis=0, keepdims=True)
    small[...] = jnp.zeros_like(small)
    small[8:16, :] = rates[:8]
    small[0:1, :] = gains / first_gain[...]
    small[1:2, :] = mlp_part[...]

    @pl.when(step == 0)
    def _():
        small[2:3, : dgain.shape[1]] = dgain[...]
        small[2:3, dgain.shape[1] : 2 * dgain.shape[1]] = dbias[...]

    @pl.when(step == pl.num_programs(0) - 1)
    def _():
        settle(moves, send, recv)


def dots(dproj, gathered, weight, rate, gains, mlp_part, dgain, dbias, side_a, side_b, collective_id):
    rows, width = gathered.shape
    full = lambda *shape: pl.BlockSpec(shape, lambda i: (0,) * len(shape))
    cols = lambda height: pl.BlockSpec((height, SPAN), lambda i: (0, i))
    down = lambda wide: pl.BlockSpec((SPAN, wide), lambda i: (i, 0))
    return pl.pallas_call(
        dots_kernel,
        grid=(width // SPAN,),
        in_specs=[
            full(*dproj.shape),
            cols(rows),
            down(weight.shape[1]),
            cols(rate.shape[0]),
            cols(1),
            cols(1),
            full(*dgain.shape),
            full(*dbias.shape),
            *anywhere(2),
        ],
        out_specs=[down(weight.shape[1]), cols(rows), cols(16), *anywhere(2)],
        out_shape=[
            jax.ShapeDtypeStruct(weight.shape, BF16),
            jax.ShapeDtypeStruct((rows, width), BF16),
            jax.ShapeDtypeStruct((16, width), F32),
            *[jax.ShapeDtypeStruct(side_a.shape, BF16)] * 2,
        ],
        scratch_shapes=sem_pair(2),
        compiler_params=pltpu.CompilerParams(
            vmem_limit_bytes=VMEM_MOST, collective_id=collective_id, has_side_effects=True
        ),
        cost_estimate=pl.CostEstimate(
            flops=4 * rows * width * dproj.shape[1], bytes_accessed=24 * 1024 * 1024, transcendentals=0
        ),
        name="dots",
    )(dproj, gathered, weight, rate, gains, mlp_part, dgain, dbias, side_a, side_b)


def finish_kernel(*refs):
    own_gu, far_gu, own_down, far_down, in_ref, out_ref = refs[:6]
    tokens, hidden, d_hidden, gain, plane_total, back_own, back_got = refs[6:13]
    small, sums, init_in = refs[13:16]
    gu, down, in_out, out_out, result, d_tokens = refs[16:22]
    first, second, mix_gain, mix_bias, d_rate, d_init = refs[22:]

    @pl.when(pl.program_id(0) == 0)
    def _():
        local = mix_gain.shape[1]
        first[...] = sums[0:1, :]
        second[...] = sums[1:2, :]
        mix_gain[...] = small[2:3, :local]
        mix_bias[...] = small[2:3, local : 2 * local]
        d_rate[...] = small[8 : 8 + d_rate.shape[0], :]
        d_init[...] = init_in[...]

    gu[...] = own_gu[...].astype(F32) + far_gu[...].astype(F32)
    down[...] = own_down[...].astype(F32) + far_down[...].astype(F32)
    width = in_out.shape[2]
    for part in range(4):
        in_out[:, part, :] = in_ref[:, part * width : (part + 1) * width].astype(F32)
    out_out[...] = out_ref[...].astype(F32)
    d_normed = back_own[...].astype(F32)
    for at in range(3):
        d_normed = d_normed + back_got[at].astype(F32)
    result[...] = (hidden[...] + plane_total[...]).astype(BF16)
    source = tokens[...].astype(F32)
    d_tokens[...] = d_hidden[...] + norm_back(source, rms_scale(source), gain[...], d_normed)


def finish(own_gu, far_gu, own_down, far_down, in_all, out_all, tokens, hidden, d_hidden, gain, plane_total, backs, small, sums, init, local):
    units, width = own_down.shape
    tall, wide = in_all.shape
    near = tokens.shape[0]
    steps = pl.cdiv(units, FINISH)
    rows = lambda *shape: pl.BlockSpec(shape, lambda i: (i,) + (0,) * (len(shape) - 1))
    few = near // steps
    full = lambda *shape: pl.BlockSpec(shape, lambda i: (0,) * len(shape))
    little = [(1, width), (1, width), (1, local), (1, local), (init.shape[0], width), init.shape]
    return pl.pallas_call(
        finish_kernel,
        grid=(steps,),
        in_specs=[tile(2, FINISH, width)] * 2
        + [tile(FINISH, width)] * 2
        + [rows(tall // steps, wide), rows(out_all.shape[0] // steps, width)]
        + [rows(few, width)] * 3
        + [pl.BlockSpec((1, width), lambda i: (0, 0)), rows(few, width)]
        + [rows(few, width), tile(3, few, width)]
        + [full(*small.shape), full(*sums.shape), full(*init.shape)],
        out_specs=[
            tile(2, FINISH, width),
            tile(FINISH, width),
            rows(tall // steps, 4, wide // 4),
            rows(out_all.shape[0] // steps, width),
            rows(few, width),
            rows(few, width),
            *[full(*shape) for shape in little],
        ],
        out_shape=[
            jax.ShapeDtypeStruct((2, units, width), F32),
            jax.ShapeDtypeStruct((units, width), F32),
            jax.ShapeDtypeStruct((tall, 4, wide // 4), F32),
            jax.ShapeDtypeStruct(out_all.shape, F32),
            jax.ShapeDtypeStruct((near, width), BF16),
            jax.ShapeDtypeStruct((near, width), F32),
            *[jax.ShapeDtypeStruct(shape, F32) for shape in little],
        ],
        compiler_params=pltpu.CompilerParams(vmem_limit_bytes=VMEM_MOST),
        cost_estimate=pl.CostEstimate(
            flops=3 * units * width, bytes_accessed=24 * units * width, transcendentals=0
        ),
        name="finish",
    )(own_gu, far_gu, own_down, far_down, in_all, out_all, tokens, hidden, d_hidden, gain, plane_total, *backs, small, sums, init)


PIECE = 2048


def rms_scale(values):
    return lax.rsqrt(jnp.mean(values * values, axis=-1, keepdims=True) + 1e-06)


def norm_back(values, row_scale, gains, upstream):
    weighted = upstream * gains
    return row_scale * weighted - values * row_scale**3 * jnp.mean(
        weighted * values, axis=-1, keepdims=True
    )


def contract_rows(left, right):
    return lax.dot_general(
        left, right, (((0,), (0,)), ((), ())), preferred_element_type=jnp.float32
    )


def contract_cols(left, right):
    return lax.dot_general(
        left, right, (((1,), (1,)), ((), ())), preferred_element_type=jnp.float32
    )


def after(values, *others):
    return lax.optimization_barrier((values, *others))[0]


def swap_core(values):
    size = lax.axis_size("head")
    return lax.ppermute(values, "head", [(at, at ^ 1) for at in range(size)])


def shift_chip(values, hops):
    size = lax.axis_size("head")
    return lax.ppermute(values, "head", [(at, (at + 2 * hops) % size) for at in range(size)])


def swap_mlp(values, flip):
    size = lax.axis_size("mlp")
    return lax.ppermute(values, "mlp", [(at, at ^ flip) for at in range(size)])


def sum_small(values, axis):
    size = lax.axis_size(axis)
    flip = 1
    while flip < size:
        values = values + lax.ppermute(values, axis, [(at, at ^ flip) for at in range(size)])
        flip *= 2
    return values


def spread_mlp(values):
    return [values] + [swap_mlp(values, flip) for flip in range(1, lax.axis_size("mlp"))]


def scatter_mlp(parts):
    total = parts[0]
    for flip in range(1, len(parts)):
        total = total + swap_mlp(parts[flip].astype(BF16), flip).astype(F32)
    return total


def sum_mlp(values, shape):
    size = lax.axis_size("mlp")
    me = lax.axis_index("mlp")
    rows = values.shape[0] // size
    low = values.astype(BF16)
    total = lax.dynamic_slice_in_dim(values, me * rows, rows)
    for flip in range(1, size):
        part = lax.dynamic_slice_in_dim(low, (me ^ flip) * rows, rows)
        total = total + swap_mlp(part, flip).astype(F32)
    own = total.astype(BF16)
    whole = jnp.zeros((values.shape[0],) + shape, F32)
    start = (0,) * len(shape)
    whole = lax.dynamic_update_slice(whole, total.reshape((rows,) + shape), (me * rows,) + start)
    for flip in range(1, size):
        part = swap_mlp(own, flip).astype(F32).reshape((rows,) + shape)
        whole = lax.dynamic_update_slice(whole, part, ((me ^ flip) * rows,) + start)
    return whole


def on_device(
    tokens,
    out_grad,
    seq_lengths,
    norm_gain,
    in_weight,
    rate_weight,
    init_state,
    mix_gain,
    mix_bias,
    out_weight,
    mlp_gain,
    gate_up,
    down_weight,
):
    core = lax.axis_index("head") % 2
    chips = lax.axis_size("head") // 2
    row_total = tokens.shape[1]
    model_width = tokens.shape[2]
    local_width = in_weight.shape[2]
    head_count = init_state.shape[0]
    first_gain = norm_gain.astype(jnp.float32)
    second_gain = mlp_gain.astype(jnp.float32)
    source = tokens[0].astype(jnp.float32)
    cotangent = out_grad[0]
    first_scale = rms_scale(source)
    normed = (source * first_scale * first_gain).astype(BF16)
    gathered = lax.all_gather(normed, "head", axis=0, tiled=True)
    in_flat = jnp.concatenate(
        [
            in_weight.reshape(model_width, 4 * local_width),
            rate_weight,
            jnp.zeros((model_width, LANES - head_count), BF16),
        ],
        axis=1,
    )
    cot_plane = spread_mlp(cotangent)
    projected = jnp.dot(gathered, in_flat, preferred_element_type=jnp.float32)
    mix_gains = mix_gain.astype(jnp.float32)[None]
    mix_biases = mix_bias.astype(jnp.float32)[None]
    (mixed, *kept), _ = mixer_forward(
        seq_lengths, projected, init_state, mix_gains, mix_biases, Carry()
    )

    late_out_weight, late_cotangent, _ = lax.optimization_barrier((out_weight, cotangent, gathered))
    out_full = lax.all_gather(late_out_weight, "head", axis=0, tiled=True)
    cot_far = [shift_chip(late_cotangent, hops) for hops in range(1, chips)]
    cot_far = jnp.concatenate(cot_far, axis=0)
    cot_all = jnp.concatenate(cot_plane + spread_mlp(cot_far), axis=0)
    cot_plane = jnp.concatenate(cot_plane, axis=0)

    mixed_rows = lax.all_to_all(mixed, "head", 0, 1, tiled=True)
    branch = jnp.dot(mixed_rows, out_full, preferred_element_type=jnp.float32)
    hidden = source + branch
    second_scale = rms_scale(hidden)
    normed2 = (hidden * second_scale * second_gain).astype(BF16)

    gate_up_rows = jnp.transpose(gate_up, (1, 2, 0))
    gate_rows, up_rows = gate_up_rows[0], gate_up_rows[1]
    normed_plane = spread_mlp(normed2)
    normed_far = [shift_chip(normed2, hops) for hops in range(1, chips)]
    plane = jnp.concatenate(normed_plane, axis=0)
    gate = contract_cols(plane, gate_rows)
    up = contract_cols(plane, up_rows)
    silu, slope = gated(gate, up)
    d_act = contract_cols(cot_plane, down_weight)
    d_gate = (d_act * up * slope).astype(BF16)
    d_up = (d_act * silu).astype(BF16)
    d_plane = jnp.dot(d_gate, gate_rows, preferred_element_type=jnp.float32) + jnp.dot(
        d_up, up_rows, preferred_element_type=jnp.float32
    )
    members = lax.axis_size("mlp")
    d_normed2 = scatter_mlp([d_plane[at * row_total : (at + 1) * row_total] for at in range(members)])
    activation = (silu * up).astype(BF16)
    out_plane = jnp.dot(activation, down_weight, preferred_element_type=jnp.float32)
    mlp_out = scatter_mlp([out_plane[at * row_total : (at + 1) * row_total] for at in range(members)])
    result = (hidden + mlp_out).astype(BF16)[None]

    grad_mlp_gain = sum_small(
        sum_small(jnp.sum(d_normed2 * hidden * second_scale, axis=0), "mlp"), "head"
    )
    d_hidden = cotangent.astype(jnp.float32) + norm_back(
        hidden, second_scale, second_gain, d_normed2
    )
    d_branch = d_hidden.astype(BF16)
    d_mixed_rows = contract_cols(d_branch, out_full).astype(BF16)
    d_mixed = lax.all_to_all(d_mixed_rows, "head", 1, 0, tiled=True)
    shard_rows = lax.all_gather(d_branch, "head", axis=0, tiled=True)
    (d_projected, grad_init_state, grad_mix_gain, grad_mix_bias), _ = mixer_backward(
        seq_lengths, d_mixed, projected, init_state, mix_gains, mix_biases, kept, Carry()
    )
    grad_in_flat = contract_rows(gathered, d_projected)
    grad_in_weight = sum_mlp(grad_in_flat[:, : 4 * local_width], (4, local_width))
    d_normed = lax.psum_scatter(
        contract_cols(d_projected, in_flat).astype(BF16),
        "head",
        scatter_dimension=0,
        tiled=True,
    ).astype(jnp.float32)
    grad_out_weight = sum_mlp(contract_rows(mixed, shard_rows), (model_width,))
    small = jnp.concatenate(
        [
            grad_in_flat[:, 4 * local_width : 4 * local_width + head_count].reshape(-1),
            grad_init_state.reshape(-1),
            grad_mix_gain[0],
            grad_mix_bias[0],
        ]
    )
    small = sum_small(small, "mlp")
    sizes = [model_width * head_count, grad_init_state.size, local_width, local_width]
    ends = [sum(sizes[: at + 1]) for at in range(4)]
    grad_rate_weight = small[: ends[0]].reshape(model_width, head_count)
    grad_init_state = small[ends[0] : ends[1]].reshape(grad_init_state.shape)
    grad_mix_gain = small[ends[1] : ends[2]]
    grad_mix_bias = small[ends[2] : ends[3]]
    grad_norm_gain = sum_small(
        sum_small(jnp.sum(d_normed * source * first_scale, axis=0), "mlp"), "head"
    )
    grad_tokens = d_hidden + norm_back(source, first_scale, first_gain, d_normed)

    far, _ = lax.optimization_barrier((jnp.concatenate(normed_far, axis=0), d_normed2))
    normed_all = jnp.concatenate(normed_plane + spread_mlp(far), axis=0)
    half = model_width // 2
    pieces = max(1, normed_all.shape[0] // PIECE)
    piece = normed_all.shape[0] // pieces
    sums = None
    for at in range(pieces):
        rows_in = normed_all[at * piece : (at + 1) * piece]
        rows_cot = cot_all[at * piece : (at + 1) * piece]
        if sums is not None:
            rows_in, rows_cot, sums = lax.optimization_barrier((rows_in, rows_cot, sums))
        gate = contract_cols(rows_in, gate_rows)
        up = contract_cols(rows_in, up_rows)
        silu, slope = gated(gate, up)
        activation = (silu * up).astype(BF16)
        d_act = contract_cols(rows_cot, down_weight)
        d_gate = d_act * up * slope
        d_up = d_act * silu
        mine = jnp.where(core == 0, d_gate, d_up).astype(BF16)
        theirs = jnp.where(core == 0, d_up, d_gate).astype(BF16)
        cot_theirs = jnp.where(core == 0, rows_cot[:, half:], rows_cot[:, :half])
        cot_mine = jnp.where(core == 0, rows_cot[:, :half], rows_cot[:, half:])
        terms = [
            contract_rows(theirs, rows_in),
            contract_rows(activation, cot_theirs),
            contract_rows(mine, rows_in),
            contract_rows(activation, cot_mine),
        ]
        sums = terms if sums is None else [old + new for old, new in zip(sums, terms)]
    gate_theirs = swap_core(sums[0].astype(BF16))
    down_theirs = swap_core(sums[1].astype(BF16))
    gate_mine = sums[2] + gate_theirs.astype(F32)
    down_mine = sums[3] + down_theirs.astype(F32)
    gate_other = swap_core(gate_mine.astype(BF16)).astype(F32)
    down_other = swap_core(down_mine.astype(BF16)).astype(F32)
    grad_gate_up = jnp.stack(
        [jnp.where(core == 0, gate_mine, gate_other), jnp.where(core == 0, gate_other, gate_mine)]
    )
    grad_gate_up = jnp.transpose(grad_gate_up, (2, 0, 1))
    grad_down = jnp.concatenate(
        [jnp.where(core == 0, down_mine, down_other), jnp.where(core == 0, down_other, down_mine)],
        axis=1,
    )
    return (
        result,
        grad_tokens[None],
        grad_norm_gain,
        grad_in_weight,
        grad_rate_weight,
        grad_init_state,
        grad_mix_gain,
        grad_mix_bias,
        grad_out_weight,
        grad_mlp_gain,
        grad_gate_up,
        grad_down,
    )


def spread_kernel(*refs):
    mixed_rows, tokens, gain, out_cross, out_other, cot, cot_line = refs[:7]
    hidden, normed2, got, line, side_x, side_y = refs[7:13]
    weights, loads, send, recv = refs[13:]
    across, along = near_peers()[:2]
    half = tokens.shape[0] // 2
    top, bottom = pl.ds(0, half), pl.ds(half, half)
    direct = [(normed2, got.at[0], across), (normed2, got.at[1], along)]
    corner = [
        (got.at[0, top], got.at[2, top], along),
        (got.at[1, bottom], got.at[2, bottom], across),
    ]
    rest = line_moves(cot, 1, line) + [(cot_line, side_x, across), (cot_line, side_y, along)]
    fetch = [
        pltpu.make_async_copy(part, weights.at[at], loads.at[at])
        for at, part in enumerate((out_cross, out_other))
    ]
    for copy in fetch:
        copy.start()
    greet([across, along, *line_peers()])
    launch(rest, send.at[2], recv.at[2])
    for copy in fetch:
        copy.wait()

    def body(at, _):
        span = pl.ds(pl.multiple_of(at * SPAN, SPAN), SPAN)
        branch = mm(mixed_rows[0], weights[0, :, span]) + mm(mixed_rows[1], weights[1, :, span])
        hidden[:, span] = tokens[:, span].astype(F32) + branch
        return 0

    lax.fori_loop(0, tokens.shape[1] // SPAN, body, 0)
    values = hidden[...]
    normed2[...] = (values * rms_scale(values) * gain[:, values.shape[1] : 2 * values.shape[1]]).astype(BF16)
    launch(direct, send.at[0], recv.at[0])
    settle(direct, send.at[0], recv.at[0])
    launch(corner, send.at[1], recv.at[1])
    settle(corner, send.at[1], recv.at[1])
    settle(rest, send.at[2], recv.at[2])


def spread_plane(mixed_rows, tokens, gains, out_halves, cot, cot_line, collective_id):
    rows, width = tokens.shape
    vmem = pl.BlockSpec(memory_space=pltpu.VMEM)
    return pl.pallas_call(
        spread_kernel,
        in_specs=[vmem, vmem, vmem, *anywhere(4)],
        out_specs=[vmem, vmem, *anywhere(4)],
        out_shape=[
            jax.ShapeDtypeStruct((rows, width), F32),
            jax.ShapeDtypeStruct((rows, width), BF16),
            jax.ShapeDtypeStruct((3, rows, width), BF16),
            *[jax.ShapeDtypeStruct((3 * rows // 2, width), BF16)] * 3,
        ],
        scratch_shapes=[
            pltpu.VMEM((2, width // 2, width), BF16),
            pltpu.SemaphoreType.DMA((2,)),
            pltpu.SemaphoreType.DMA((3, 5)),
            pltpu.SemaphoreType.DMA((3, 5)),
        ],
        compiler_params=pltpu.CompilerParams(
            vmem_limit_bytes=VMEM_MOST, collective_id=collective_id, has_side_effects=True
        ),
        cost_estimate=pl.CostEstimate(
            flops=2 * rows * width * width, bytes_accessed=3 * width * width, transcendentals=0
        ),
        name="spread_plane",
    )(mixed_rows, tokens, gains, *out_halves, cot, cot_line)


class PlaneSum:
    def __init__(self, parts, bufs, send, recv, loads):
        self.parts = parts
        self.got, self.own, self.passed, self.kept, self.late = bufs
        self.send, self.recv, self.loads = send, recv, loads
        self.across, self.along = near_peers()[:2]
        half = parts.shape[1] // 2
        self.spans = (pl.ds(0, half), pl.ds(half, half))

    def moves(self, phase):
        top, bottom = self.spans
        if phase == 0:
            return [
                (self.parts.at[1, top], self.got.at[0], self.across),
                (self.parts.at[3, top], self.got.at[1], self.across),
                (self.parts.at[2, bottom], self.got.at[2], self.along),
                (self.parts.at[3, bottom], self.got.at[3], self.along),
            ]
        return [
            (self.passed.at[0], self.late.at[0], self.along),
            (self.passed.at[1], self.late.at[1], self.across),
        ]

    def begin(self):
        launch(self.moves(0), self.send.at[0], self.recv.at[0])

    def middle(self):
        top, bottom = self.spans
        gather_parts(
            [
                (self.parts.at[0, top], self.own.at[0]),
                (self.parts.at[2, top], self.own.at[1]),
                (self.parts.at[0, bottom], self.own.at[2]),
                (self.parts.at[1, bottom], self.own.at[3]),
            ],
            self.loads,
        )
        settle(self.moves(0), self.send.at[0], self.recv.at[0])
        for half in range(2):
            self.passed[half] = (
                self.own[2 * half + 1].astype(F32) + self.got[2 * half + 1].astype(F32)
            ).astype(BF16)
        launch(self.moves(1), self.send.at[1], self.recv.at[1])
        for half in range(2):
            self.kept[half] = self.own[2 * half].astype(F32) + self.got[2 * half].astype(F32)

    def finish(self, target):
        settle(self.moves(1), self.send.at[1], self.recv.at[1])
        for half in range(2):
            target[self.spans[half], :] = self.kept[half] + self.late[half].astype(F32)


def plane_buffers(rows, width):
    half = rows // 2
    return [
        pltpu.VMEM((4, half, width), BF16),
        pltpu.VMEM((4, half, width), BF16),
        pltpu.VMEM((2, half, width), BF16),
        pltpu.VMEM((2, half, width), F32),
        pltpu.VMEM((2, half, width), BF16),
    ]


def turn_kernel(*refs):
    d_plane, out_plane, normed2, out_cross, out_other, hidden, cot, gain = refs[:8]
    d_mixed, line, d_hidden, d_branch, mlp_part, plane_total = refs[8:14]
    d_bufs, out_bufs, weights, slots, d_normed = refs[14:19], refs[19:24], refs[24], refs[25], refs[26]
    sum_send, sum_recv, loads, row_send, row_recv, line_send, line_recv = refs[27:]
    me = lax.axis_index("head")
    chip, core = me // 2, lax.rem(me, 2)
    rows = hidden.shape[0]
    width = slots.shape[2]
    d_sum = PlaneSum(d_plane, d_bufs, sum_send.at[0], sum_recv.at[0], loads)
    out_sum = PlaneSum(out_plane, out_bufs, sum_send.at[1], sum_recv.at[1], loads)
    line_copies = line_moves(normed2, 1, line)
    fetch = [
        pltpu.make_async_copy(part, weights.at[at], loads.at[4 + at])
        for at, part in enumerate((out_cross, out_other))
    ]
    greet([d_sum.across, d_sum.along] + [head_peer(at) for at in range(1, 8)])
    d_sum.begin()
    launch(line_copies, line_send, line_recv)
    for copy in fetch:
        copy.start()
    d_sum.middle()
    d_sum.finish(d_normed)
    out_sum.begin()
    scale = rms_scale(hidden[...])
    part = d_normed[...]
    mlp_part[...] = jnp.sum(part * hidden[...] * scale, axis=0, keepdims=True)
    gains = gain[:, part.shape[1] : 2 * part.shape[1]]
    total = cot[...].astype(F32) + norm_back(hidden[...], scale, gains, part)
    d_hidden[...] = total
    d_branch[...] = total.astype(BF16)
    for copy in fetch:
        copy.wait()

    def row_copy(at, ahead, sender, target, local):
        place = d_mixed.at[pl.ds(pl.multiple_of(me * rows, rows), rows)]
        if local:
            return pltpu.make_async_copy(slots.at[at], place, row_send.at[at])
        return pltpu.make_async_remote_copy(
            src_ref=slots.at[at],
            dst_ref=place,
            send_sem=row_send.at[at],
            recv_sem=row_recv.at[ahead],
            device_id={"head": target},
            device_id_type=MESH,
        )

    order = (4, 3, 5, 2, 6, 1, 7, 0)
    for at, ahead in enumerate(order):
        target = lax.rem(me + ahead, 8)
        columns = pl.ds(pl.multiple_of(target // 2 * width, width), width)
        slots[at] = mm_nt(d_branch[...], weights[ahead % 2, columns, :]).astype(BF16)
        row_copy(at, ahead, me, target, ahead == 0).start()
    out_sum.middle()
    for at, ahead in enumerate(order):
        copy = row_copy(at, ahead, me, lax.rem(me + ahead, 8), ahead == 0)
        copy.wait()
    out_sum.finish(plane_total)
    settle(line_copies, line_send, line_recv)


def turn(d_plane, out_plane, normed2, out_halves, hidden, cot, gains, local_width, collective_id):
    rows, width = normed2.shape
    vmem = pl.BlockSpec(memory_space=pltpu.VMEM)
    return pl.pallas_call(
        turn_kernel,
        in_specs=anywhere(5) + [vmem] * 3,
        out_specs=anywhere(2) + [vmem] * 4,
        out_shape=[
            jax.ShapeDtypeStruct((8 * rows, local_width), BF16),
            jax.ShapeDtypeStruct((3 * rows // 2, width), BF16),
            jax.ShapeDtypeStruct((rows, width), F32),
            jax.ShapeDtypeStruct((rows, width), BF16),
            jax.ShapeDtypeStruct((1, width), F32),
            jax.ShapeDtypeStruct((rows, width), F32),
        ],
        scratch_shapes=[
            *plane_buffers(rows, width),
            *plane_buffers(rows, width),
            pltpu.VMEM((2, width // 2, width), BF16),
            pltpu.VMEM((8, rows, local_width), BF16),
            pltpu.VMEM((rows, width), F32),
            pltpu.SemaphoreType.DMA((2, 2, 4)),
            pltpu.SemaphoreType.DMA((2, 2, 4)),
            pltpu.SemaphoreType.DMA((6,)),
            *sem_pair(8),
            *sem_pair(3),
        ],
        compiler_params=pltpu.CompilerParams(
            vmem_limit_bytes=VMEM_MOST, collective_id=collective_id, has_side_effects=True
        ),
        cost_estimate=pl.CostEstimate(
            flops=2 * rows * width * width, bytes_accessed=4 * width * width, transcendentals=0
        ),
        name="turn",
    )(d_plane, out_plane, normed2, *out_halves, hidden, cot, gains)


def halves_of(values):
    half = values.shape[0] // 2
    return pl.ds(0, half), pl.ds(half, half)


def sides_and_line(ins, outs):
    across, along = near_peers()[:2]
    top, bottom = halves_of(outs[2])
    moves = [
        (ins[0], outs[0], across),
        (ins[0], outs[1], along),
        (ins[1].at[top], outs[2].at[top], along),
        (ins[2].at[bottom], outs[2].at[bottom], across),
    ]
    return [across, along, *line_peers()], moves + line_moves(ins[3], 0, outs[4])


def corner_rest(ins, outs):
    across, along = near_peers()[:2]
    top, bottom = halves_of(outs[3])
    return [
        (outs[0].at[top], outs[3].at[top], along),
        (outs[1].at[bottom], outs[3].at[bottom], across),
    ]


def sides(ins, outs):
    near = near_peers()[:2]
    return near, [(ins[at // 2], outs[at], near[at % 2]) for at in range(4)]


def on_square(
    tokens,
    out_grad,
    seq_lengths,
    norm_gain,
    in_weight,
    rate_weight,
    init_state,
    mix_gain,
    mix_bias,
    out_weight,
    mlp_gain,
    gate_up,
    down_weight,
):
    heads = lax.axis_size("head")
    rows = tokens.shape[1]
    model_width = tokens.shape[2]
    local_width = in_weight.shape[2]
    head_count = init_state.shape[0]
    vectors = [part.reshape(-1, LANES) for part in (norm_gain, mlp_gain, mix_gain, mix_bias)]
    source = tokens[0]
    cotangent = out_grad[0]
    far_shape = (3 * rows // 2, model_width)
    (projected, rate_rows), (mixed, *kept), gains, moved = head(
        seq_lengths, source, rate_weight.T, init_state, vectors, in_weight, cotangent, out_weight, 0
    )
    gathered, cot_got, in_main, mixed_rows, out_cross, out_other, cot_line_a = moved
    out_halves = [part.reshape(model_width // 2, model_width) for part in (out_cross, out_other)]
    hidden, normed2, normed_got, cot_line_b, cot_x_a, cot_y_a = spread_plane(
        mixed_rows, source, gains, out_halves, cotangent, cot_line_a, 3
    )
    gate_up_rows = jnp.transpose(gate_up, (1, 2, 0))
    (d_plane, out_plane), plane_acts, moved = mlp_plane(
        normed2,
        normed_got,
        cotangent,
        cot_got,
        gate_up_rows,
        down_weight,
        Carry(
            [cot_line_b, cot_x_a, cot_y_a, normed2],
            [far_shape] * 5,
            sides_and_line,
            9,
            4,
            (1, 2, corner_rest),
        ),
    )
    cot_x_b, cot_y_b, cot_corner_a, cot_corner_b, normed_line_a = moved
    d_mixed, normed_line_b, d_hidden, d_branch, mlp_part, plane_total = turn(
        d_plane,
        out_plane,
        normed2,
        out_halves,
        hidden,
        cotangent,
        gains,
        local_width,
        5,
    )
    shard_rows = lax.all_gather(after(d_branch, d_mixed), "head", axis=0, tiled=True)
    (d_projected, grad_init_state, grad_mix_gain, grad_mix_bias), normed_sides = mixer_backward(
        seq_lengths,
        d_mixed,
        projected,
        init_state,
        gains,
        gains,
        kept,
        Carry([normed_line_a, normed_line_b], [far_shape] * 4, sides, 4, 7),
        (2 * model_width // local_width, 2 * model_width // local_width + 1),
    )
    in_part, back_part, small, normed_corner_a, normed_corner_b = dots(
        d_projected,
        gathered,
        in_main,
        rate_rows,
        gains,
        mlp_part,
        grad_mix_gain,
        grad_mix_bias,
        normed_sides[0],
        normed_sides[3],
        8,
    )
    out_part = contract_rows(mixed, after(shard_rows, in_part)).astype(BF16)
    cot_far = [cot_line_a, cot_line_b, cot_x_a, cot_x_b, cot_y_a, cot_y_b]
    normed_far = [normed_line_a, normed_line_b]
    normed_far += [normed_sides[0], normed_sides[2], normed_sides[1], normed_sides[3]]
    grads, back_got, back_own, small, sums, grad_init_state = mlp_grads(
        (normed2, normed_got, [*normed_far, normed_corner_a, normed_corner_b]),
        (cotangent, cot_got, [*cot_far, cot_corner_a, cot_corner_b]),
        in_part,
        out_part,
        back_part.reshape(heads // 2, 2, rows, model_width),
        gate_up_rows,
        down_weight,
        plane_acts,
        small,
        grad_init_state,
        9,
    )
    own_gate_up, own_down, other_gate_up, other_down, in_all, out_all = grads
    done = finish(
        own_gate_up,
        other_gate_up,
        own_down,
        other_down,
        in_all.reshape(in_main.shape),
        out_all.reshape(out_weight.shape),
        tokens[0],
        hidden,
        d_hidden,
        gains,
        plane_total,
        (back_own, back_got),
        small,
        sums,
        grad_init_state,
        local_width,
    )
    grad_gate_up, grad_down, grad_in_weight, grad_out_weight, result, grad_tokens = done[:6]
    grad_norm_gain, grad_mlp_gain, grad_mix_gain, grad_mix_bias, grad_rate, grad_init_state = done[6:]
    grad_gate_up = jnp.transpose(grad_gate_up, (2, 0, 1))
    return (
        result[None],
        grad_tokens[None],
        grad_norm_gain[0],
        grad_in_weight,
        grad_rate.T,
        grad_init_state,
        grad_mix_gain[0],
        grad_mix_bias[0],
        grad_out_weight,
        grad_mlp_gain[0],
        grad_gate_up,
        grad_down,
    )


def solution(mesh):
    square = mesh.shape["mlp"] == 4 and mesh.shape["head"] == 8
    return jax.shard_map(
        on_square if square else on_device,
        mesh=mesh,
        in_specs=(
            P("mlp", "head", None),
            P("mlp", "head", None),
            P("mlp", None),
            P(),
            P(None, None, "head"),
            P(None, "head"),
            P("head", None, None),
            P("head"),
            P("head"),
            P("head", None),
            P(),
            P(None, None, "mlp"),
            P("mlp", None),
        ),
        out_specs=(
            P("mlp", "head", None),
            P("mlp", "head", None),
            P(),
            P(None, None, "head"),
            P(None, "head"),
            P("head", None, None),
            P("head"),
            P("head"),
            P("head", None),
            P(),
            P(None, None, "mlp"),
            P("mlp", None),
        ),
        check_vma=False,
    )
```
